32 devices in a mesh: dp: 16 (over z, x, core), tensor: 2 (over y).
Axes of the slice: x: 2, y: 2, z: 4, core: 2. Of those that a mesh axis runs over, the one named last changes fastest.
Arguments:
- clean_images: bfloat16 [64, 256, 768], P(('dp', 'tensor')), may hold values from -6 to 6
- noise_draw: bfloat16 [64, 256, 768], P(('dp', 'tensor')), may hold values from -6 to 6
- levels: int32 [64], P(('dp', 'tensor')), may hold values from 0 to 999
- labels: int32 [64], P(('dp', 'tensor')), may hold values from 0 to 999
- dropped: int32 [64], P(('dp', 'tensor')), may hold values 0 or 1
- groups: int32 [64], P(('dp', 'tensor')), may hold values from 0 to 3
- step_count: int32 [1], replicated, may hold values from 1 to 20
- inward: float32 [1024, 3, 1024], P('dp', None, 'tensor'), may hold values from -0.1875 to 0.1875
- first_inward: float32 [1024, 3, 1024], P('dp', None, 'tensor'), may hold values from -2.744419e-06 to 2.744419e-06, as said below
- second_inward: float32 [1024, 3, 1024], P('dp', None, 'tensor'), may hold values from 3.347482e-12 to 1.3389928e-11
- outward: float32 [1024, 1024], P('tensor', 'dp'), may hold values from -0.75 to 0.75
- first_outward: float32 [1024, 1024], P('tensor', 'dp'), may hold values from -1.3722094e-06 to 1.3722094e-06, as said below
- second_outward: float32 [1024, 1024], P('tensor', 'dp'), may hold values from 8.368705e-13 to 3.347482e-12
- expand: float32 [1024, 2, 3072], P('dp', None, 'tensor'), may hold values from -0.1875 to 0.1875
- first_expand: float32 [1024, 2, 3072], P('dp', None, 'tensor'), may hold values from -1.029157e-06 to 1.029157e-06, as said below
- second_expand: float32 [1024, 2, 3072], P('dp', None, 'tensor'), may hold values from 4.7073966e-13 to 1.8829586e-12
- shrink: float32 [3072, 1024], P('tensor', 'dp'), may hold values from -0.109375 to 0.109375
- first_shrink: float32 [3072, 1024], P('tensor', 'dp'), may hold values from -2.744419e-06 to 2.744419e-06, as said below
- second_shrink: float32 [3072, 1024], P('tensor', 'dp'), may hold values from 3.347482e-12 to 1.3389928e-11
- patches: float32 [2, 768, 1024], P(None, ('dp', 'tensor')), may hold values from -0.1875 to 0.1875
- first_patches: float32 [2, 768, 1024], P(None, ('dp', 'tensor')), may hold values from -6.861047e-06 to 6.861047e-06, as said below
- second_patches: float32 [2, 768, 1024], P(None, ('dp', 'tensor')), may hold values from 2.0921763e-11 to 8.368705e-11
- classes: float32 [1001, 768], P(None, ('dp', 'tensor')), may hold values from -0.21875 to 0.21875
- first_classes: float32 [1001, 768], P(None, ('dp', 'tensor')), may hold values from -6.861047e-06 to 6.861047e-06, as said below
- second_classes: float32 [1001, 768], P(None, ('dp', 'tensor')), may hold values from 2.0921763e-11 to 8.368705e-11
- mapping: float32 [768, 4096], P(('dp', 'tensor')), may hold values from -0.21875 to 0.21875
- first_mapping: float32 [768, 4096], P(('dp', 'tensor')), may hold values from -6.861047e-06 to 6.861047e-06, as said below
- second_mapping: float32 [768, 4096], P(('dp', 'tensor')), may hold values from 2.0921763e-11 to 8.368705e-11
Outputs:
- total_loss: float32 [], replicated
- grad_norm: float32 [], replicated
- inward_next: float32 [1024, 3, 1024], P('dp', None, 'tensor')
- moment_inward: float32 [1024, 3, 1024], P('dp', None, 'tensor')
- square_inward: float32 [1024, 3, 1024], P('dp', None, 'tensor')
- outward_next: float32 [1024, 1024], P('tensor', 'dp')
- moment_outward: float32 [1024, 1024], P('tensor', 'dp')
- square_outward: float32 [1024, 1024], P('tensor', 'dp')
- expand_next: float32 [1024, 2, 3072], P('dp', None, 'tensor')
- moment_expand: float32 [1024, 2, 3072], P('dp', None, 'tensor')
- square_expand: float32 [1024, 2, 3072], P('dp', None, 'tensor')
- shrink_next: float32 [3072, 1024], P('tensor', 'dp')
- moment_shrink: float32 [3072, 1024], P('tensor', 'dp')
- square_shrink: float32 [3072, 1024], P('tensor', 'dp')
- patches_next: float32 [2, 768, 1024], P(None, ('dp', 'tensor'))
- moment_patches: float32 [2, 768, 1024], P(None, ('dp', 'tensor'))
- square_patches: float32 [2, 768, 1024], P(None, ('dp', 'tensor'))
- classes_next: float32 [1001, 768], P(None, ('dp', 'tensor'))
- moment_classes: float32 [1001, 768], P(None, ('dp', 'tensor'))
- square_classes: float32 [1001, 768], P(None, ('dp', 'tensor'))
- mapping_next: float32 [768, 4096], P(('dp', 'tensor'))
- moment_mapping: float32 [768, 4096], P(('dp', 'tensor'))
- square_mapping: float32 [768, 4096], P(('dp', 'tensor'))
The draws below stay inside these ranges and needn't reach their ends.
Inputs may be any that keep to these rules, and one draw needn't show every extreme that they name: `first_inward`: entries of both signs. `first_outward`: entries of both signs. `first_expand`: entries of both signs. `first_shrink`: entries of both signs. `first_patches`: entries of both signs. `first_classes`: entries of both signs. `first_mapping`: entries of both signs.
All inputs are finite; a program needn't handle non-finite values. No bound on the sum of `dropped` on one device may be relied on, other than what follows from the above.
Results may differ from the reference program's by a relative error of at most 0.012.
Values may be sent and summed in bfloat16 or wider, within the bound.
No kernel may reach another device: no remote copies, remote signals or barrier semaphores. Data moves between devices by JAX's collectives and lax.ppermute only.
A program may use at most 256 MiB of HBM per device.

```python
import math
import jax
import jax.numpy as jnp
from jax import lax

D = 1024
HEADS = 16
HEAD_DIM = 64
FF = 3072
CD = 768
CLASSES = 1001
PD = 768
FOUR = 256
SEQ = 256
GROUPS = 4
NLEVELS = 1000
IMG_DEV = 2
IMAGES = 64
PARAMS = 19118848
N_TENSOR = 2


def grad_size(factor):
    return factor * 0.02 / math.sqrt(PARAMS)


def first_moment(key, shape, factor):
    signs = jnp.where(jax.random.bernoulli(jax.random.fold_in(key, 1), 0.5, shape), 1.0, -1.0)
    sizes = jax.random.uniform(jax.random.fold_in(key, 2), shape, jnp.float32, 0.5, 1.5)
    return (signs * sizes * grad_size(factor)).astype(jnp.float32)


def second_moment(key, shape, factor):
    size = grad_size(factor)
    spread = jnp.exp(jax.random.uniform(jax.random.fold_in(key, 3), shape, jnp.float32, 0.0, math.log(4.0)))
    return (spread * (size * size)).astype(jnp.float32)


def draw_first_inward(key, part):
    return first_moment(key, (D, 3, D), 0.4)


def draw_second_inward(key, part):
    return second_moment(key, (D, 3, D), 0.4)


def draw_first_outward(key, part):
    return first_moment(key, (D, D), 0.2)


def draw_second_outward(key, part):
    return second_moment(key, (D, D), 0.2)


def draw_first_expand(key, part):
    return first_moment(key, (D, 2, FF), 0.15)


def draw_second_expand(key, part):
    return second_moment(key, (D, 2, FF), 0.15)


def draw_first_shrink(key, part):
    return first_moment(key, (FF, D), 0.4)


def draw_second_shrink(key, part):
    return second_moment(key, (FF, D), 0.4)


def draw_first_patches(key, part):
    return first_moment(key, (2, PD, D), 1.0)


def draw_second_patches(key, part):
    return second_moment(key, (2, PD, D), 1.0)


def draw_first_classes(key, part):
    return first_moment(key, (CLASSES, CD), 1.0)


def draw_second_classes(key, part):
    return second_moment(key, (CLASSES, CD), 1.0)


def draw_first_mapping(key, part):
    return first_moment(key, (CD, FOUR + CD + 3 * D), 1.0)


def draw_second_mapping(key, part):
    return second_moment(key, (CD, FOUR + CD + 3 * D), 1.0)


def with_ends(array, own_key, low, high):
    place = [jax.random.randint(jax.random.fold_in(own_key, axis), (), 0, length) for axis, length in enumerate(array.shape)]
    main_axis = array.shape.index(max(array.shape))
    neighbour = place[:main_axis] + [(place[main_axis] + 1) % array.shape[main_axis]] + place[main_axis + 1:]
    return array.at[tuple(place)].set(low).at[tuple(neighbour)].set(high)


def level_of(rng, extent, shards, smallest, largest):
    def one(axis_at, shards_of):
        steps = jax.random.uniform(jax.random.fold_in(jax.random.fold_in(rng, 6), axis_at), (shards_of,), jnp.float32, smallest / len(shards), largest / len(shards))
        return jnp.repeat(jnp.exp(steps), extent[axis_at] // shards_of).reshape((-1,) + (1,) * (len(extent) - axis_at - 1))

    loudness = one(*shards[0])
    for cut in shards[1:]:
        loudness = loudness * one(*cut)
    return loudness


def gaussian(key, dims, scale, reach, pieces=(), held_as=jnp.bfloat16):
    array = jax.random.normal(key, dims, jnp.float32) * scale
    if len(pieces) > 0:
        array = level_of(key, dims, pieces, -0.22, 0.18) * array
    return jnp.clip(array, min=-reach, max=reach).astype(held_as)


def setup_inputs(seed: int = 0) -> dict:
    key_of = jax.random.split(jax.random.key(seed), 29)
    return {
        "clean_images": gaussian(key_of[0], (IMAGES, SEQ, PD), 1.0, 6.0, ((0, 32),)),
        "noise_draw": gaussian(key_of[1], (IMAGES, SEQ, PD), 1.0, 6.0, ((0, 32),)),
        "levels": with_ends(jax.random.randint(key_of[2], (IMAGES,), 0, NLEVELS), jax.random.fold_in(key_of[2], 1), 0, NLEVELS - 1).astype(jnp.int32),
        "labels": with_ends(jax.random.randint(key_of[3], (IMAGES,), 0, CLASSES - 1), jax.random.fold_in(key_of[3], 1), 0, (CLASSES - 1) - 1).astype(jnp.int32),
        "dropped": with_ends((jax.random.randint(key_of[4], (IMAGES,), 0, 10) < 1).astype(jnp.int32), jax.random.fold_in(key_of[4], 1), 0, 1),
        "groups": with_ends(jax.random.randint(key_of[5], (IMAGES,), 0, GROUPS), jax.random.fold_in(key_of[5], 1), 0, GROUPS - 1).astype(jnp.int32),
        "step_count": jax.random.randint(key_of[6], (1,), 1, 21).astype(jnp.int32),
        "inward": gaussian(key_of[7], (D, 3, D), D ** -0.5, 0.1875, ((0, 16), (2, 2)), jnp.float32),
        "first_inward": draw_first_inward(jax.random.fold_in(key_of[28], 71), 0),
        "second_inward": draw_second_inward(jax.random.fold_in(key_of[28], 71), 0),
        "outward": gaussian(key_of[10], (D, D), (D // 16) ** -0.5, 0.75, ((0, 2), (1, 16)), jnp.float32),
        "first_outward": draw_first_outward(jax.random.fold_in(key_of[28], 71), 0),
        "second_outward": draw_second_outward(jax.random.fold_in(key_of[28], 71), 0),
        "expand": gaussian(key_of[13], (D, 2, FF), D ** -0.5, 0.1875, ((0, 16), (2, 2)), jnp.float32),
        "first_expand": draw_first_expand(jax.random.fold_in(key_of[28], 71), 0),
        "second_expand": draw_second_expand(jax.random.fold_in(key_of[28], 71), 0),
        "shrink": gaussian(key_of[16], (FF, D), FF ** -0.5, 0.109375, ((0, 2), (1, 16)), jnp.float32),
        "first_shrink": draw_first_shrink(jax.random.fold_in(key_of[28], 71), 0),
        "second_shrink": draw_second_shrink(jax.random.fold_in(key_of[28], 71), 0),
        "patches": gaussian(key_of[19], (2, PD, D), D ** -0.5, 0.1875, ((1, 32),), jnp.float32),
        "first_patches": draw_first_patches(jax.random.fold_in(key_of[28], 71), 0),
        "second_patches": draw_second_patches(jax.random.fold_in(key_of[28], 71), 0),
        "classes": gaussian(key_of[22], (CLASSES, CD), CD ** -0.5, 0.21875, ((1, 32),), jnp.float32),
        "first_classes": draw_first_classes(jax.random.fold_in(key_of[28], 71), 0),
        "second_classes": draw_second_classes(jax.random.fold_in(key_of[28], 71), 0),
        "mapping": gaussian(key_of[25], (CD, FOUR + CD + 3 * D), CD ** -0.5, 0.21875, ((0, 32),), jnp.float32),
        "first_mapping": draw_first_mapping(jax.random.fold_in(key_of[28], 71), 0),
        "second_mapping": draw_second_mapping(jax.random.fold_in(key_of[28], 71), 0),
    }


@jax.custom_vjp
def low(v):
    return lax.optimization_barrier(v.astype(jnp.bfloat16)).astype(jnp.float32)

@jax.custom_vjp
def low_back(v):
    return v

def low_keep(v):
    return (low(v), None)

def low_pass(kept, grad):
    return (grad,)

def back_keep(v):
    return (v, None)

def back_low(kept, grad):
    return (low(grad),)
low.defvjp(low_keep, low_pass)
low_back.defvjp(back_keep, back_low)
HIGH = lax.Precision.HIGHEST
SIGMA_DATA = 0.5
LEARN_RATE = 0.05
DECAY = 0.1
BETA_ONE = 0.5
BETA_TWO = 0.5
ADAM_EPS = 1e-08
CLIP = 0.02
NORM_EPS = 1e-06

def rms_norm(value):
    return value * lax.rsqrt(lax.optimization_barrier(jnp.mean(value * value, axis=-1, keepdims=True)) + NORM_EPS)

def einsum_high(form, left, right):
    return jnp.einsum(form, left, right, precision=HIGH)

def noise_terms(levels):
    log_sigma = -3.0 + 6.0 * levels.astype(jnp.float32) / (NLEVELS - 1)
    sigma = jnp.exp(log_sigma)
    radius = jnp.sqrt(sigma * sigma + SIGMA_DATA * SIGMA_DATA)
    half = FOUR // 2
    freqs = jnp.exp(-2.0 + 4.0 * jnp.arange(half, dtype=jnp.float32) / (half - 1))
    angles = 2.0 * math.pi * (log_sigma / 4.0)[:, None] * freqs[None, :]
    return (sigma, radius, jnp.concatenate([jnp.cos(angles), jnp.sin(angles)], axis=1))

def map_forward(feats, onehot, table, mats):
    cond_zero = jnp.dot(onehot, table, precision=HIGH) + jnp.dot(low(feats), mats[:, :FOUR].T, precision=HIGH)
    inner = jnp.dot(low(rms_norm(cond_zero)), mats[:, FOUR:FOUR + CD], precision=HIGH)
    cond = cond_zero + jax.nn.gelu(inner)
    return 1.0 + jnp.dot(low(cond), mats[:, FOUR + CD:], precision=HIGH)

def row_loss(weights, row):
    inward, outward, expand, shrink, patches, classes, mapping = weights
    clean, noise, levels, labels, dropped, groups = row
    images = clean.shape[0]
    sigma, radius, feats = noise_terms(levels)
    chosen = jnp.where(dropped == 1, CLASSES - 1, labels)
    onehot = (chosen[:, None] == jnp.arange(CLASSES)[None, :]).astype(jnp.float32)
    scales = map_forward(feats, onehot, classes, mapping).reshape(images, 3, D)
    sig = sigma[:, None, None]
    rad = radius[:, None, None]
    inputs = low((clean + sig * noise) / rad)
    target = (sig * clean - SIGMA_DATA * SIGMA_DATA * noise) / (SIGMA_DATA * rad)
    resid_zero = low_back(einsum_high('isp,pd->isd', inputs, patches[0]))
    normed = low(rms_norm(resid_zero) * scales[:, None, 0])
    project = low(low_back(einsum_high('isd,dke->iske', normed, inward)))
    queries = project[:, :, 0].reshape(images, SEQ, HEADS, HEAD_DIM)
    keys = project[:, :, 1].reshape(images, SEQ, HEADS, HEAD_DIM)
    values = project[:, :, 2].reshape(images, SEQ, HEADS, HEAD_DIM)
    scores = low_back(einsum_high('iqhe,ikhe->ihqk', queries, keys) / math.sqrt(HEAD_DIM))
    probs = low(jax.nn.softmax(scores, axis=-1))
    mixed = low(low_back(einsum_high('ihqk,ikhe->iqhe', probs, values))).reshape(images, SEQ, D)
    resid_one = resid_zero + low_back(einsum_high('isd,de->ise', mixed, outward))
    normed = low(rms_norm(resid_one) * scales[:, None, 1])
    gated = low_back(einsum_high('isd,dkf->iskf', normed, expand))
    hidden = low(jax.nn.gelu(gated[:, :, 0]) * gated[:, :, 1])
    resid_two = resid_one + low_back(einsum_high('isf,fd->isd', hidden, shrink))
    last = low(rms_norm(resid_two) * scales[:, None, 2])
    output = low_back(einsum_high('isd,pd->isp', last, patches[1]))
    block = jnp.arange(images) // IMG_DEV
    same = (groups[:, None] == groups[None, :]) & (block[:, None] == block[None, :])
    weight = 1.0 / (GROUPS * lax.optimization_barrier(jnp.sum(same.astype(jnp.float32), axis=1)))
    return jnp.sum(weight * lax.optimization_barrier(jnp.mean((output - target) ** 2, axis=(1, 2))))

def reference(clean_images, noise_draw, levels, labels, dropped, groups, step_count, inward, first_inward, second_inward, outward, first_outward, second_outward, expand, first_expand, second_expand, shrink, first_shrink, second_shrink, patches, first_patches, second_patches, classes, first_classes, second_classes, mapping, first_mapping, second_mapping):
    masters = (inward, outward, expand, shrink, patches, classes, mapping)
    firsts = (first_inward, first_outward, first_expand, first_shrink, first_patches, first_classes, first_mapping)
    seconds = (second_inward, second_outward, second_expand, second_shrink, second_patches, second_classes, second_mapping)
    per_row = IMG_DEV * N_TENSOR

    def rows(value):
        return value.reshape((IMAGES // per_row, per_row) + value.shape[1:])
    data = (rows(clean_images.astype(jnp.float32)), rows(noise_draw.astype(jnp.float32)), rows(levels), rows(labels), rows(dropped), rows(groups))
    step_loss = jax.checkpoint(row_loss)

    def total(weights):
        lowered = tuple((low(w) for w in weights))

        def add(carry, row):
            return (carry + step_loss(lowered, row), None)
        result, _ = lax.scan(add, jnp.zeros((), jnp.float32), data)
        return result
    total_loss, pull = jax.vjp(total, masters)
    grads, = pull(jnp.ones_like(total_loss))
    squares = sum((jnp.sum(g * g) for g in grads))
    grad_norm = jnp.sqrt(squares)
    factor = CLIP / (grad_norm + NORM_EPS)
    count = step_count[0].astype(jnp.float32)
    fix_one = 1.0 - jnp.power(BETA_ONE, count)
    fix_two = 1.0 - jnp.power(BETA_TWO, count)
    results = []
    for master, first, second, grad in zip(masters, firsts, seconds, grads):
        clipped = grad * factor
        moment = BETA_ONE * first + (1.0 - BETA_ONE) * clipped
        square = BETA_TWO * second + (1.0 - BETA_TWO) * clipped * clipped
        step_size = moment / fix_one / (jnp.sqrt(square / fix_two) + ADAM_EPS)
        results.append((master - LEARN_RATE * (step_size + DECAY * master), moment, square))
    return (total_loss, grad_norm, results[0][0], results[0][1], results[0][2], results[1][0], results[1][1], results[1][2], results[2][0], results[2][1], results[2][2], results[3][0], results[3][1], results[3][2], results[4][0], results[4][1], results[4][2], results[5][0], results[5][1], results[5][2], results[6][0], results[6][1], results[6][2])
```

```python
import math

import jax
import jax.numpy as jnp
from jax import lax
from jax.sharding import PartitionSpec as P

D = 1024
HEAD_DIM = 64
CD = 768
CLASSES = 1001
PD = 768
FOUR = 256
SEQ = 256
GROUPS = 4
NLEVELS = 1000
LOW = jnp.bfloat16


HIGH = lax.Precision.HIGHEST
SIGMA_DATA = 0.5
LEARN_RATE = 0.05
DECAY = 0.1
BETA_ONE = 0.5
BETA_TWO = 0.5
ADAM_EPS = 1e-08
CLIP = 0.02
NORM_EPS = 1e-06


def to_low(value):
    return value.astype(LOW).astype(jnp.float32)


def rms_norm(value):
    return value * lax.rsqrt(jnp.mean(value * value, axis=-1, keepdims=True) + NORM_EPS)


def einsum_low(form, left, right):
    return jnp.einsum(form, left, right, preferred_element_type=jnp.float32)


def outer_sum(left, right):
    return jnp.dot(left.T, right, precision=HIGH)


def noise_terms(levels):
    log_sigma = -3.0 + 6.0 * levels.astype(jnp.float32) / (NLEVELS - 1)
    sigma = jnp.exp(log_sigma)
    radius = jnp.sqrt(sigma * sigma + SIGMA_DATA * SIGMA_DATA)
    half = FOUR // 2
    freqs = jnp.exp(-2.0 + 4.0 * jnp.arange(half, dtype=jnp.float32) / (half - 1))
    angles = 2.0 * math.pi * (log_sigma / 4.0)[:, None] * freqs[None, :]
    return (sigma, radius, jnp.concatenate([jnp.cos(angles), jnp.sin(angles)], axis=1))


def map_forward(feats, onehot, table, mats):
    feats_low = to_low(feats)
    cond_zero = jnp.dot(onehot, table, precision=HIGH) + jnp.dot(
        feats_low, mats[:, :FOUR].T, precision=HIGH
    )
    normed = to_low(rms_norm(cond_zero))
    inner = jnp.dot(normed, mats[:, FOUR : FOUR + CD], precision=HIGH)
    cond_low = to_low(cond_zero + jax.nn.gelu(inner))
    scales = 1.0 + jnp.dot(cond_low, mats[:, FOUR + CD :], precision=HIGH)
    return (scales, (feats_low, cond_zero, normed, inner, cond_low))


def map_backward(mats, kept, grad_scales):
    feats_low, cond_zero, normed, inner, cond_low = kept
    grad_cond = jnp.dot(grad_scales, mats[:, FOUR + CD :].T, precision=HIGH)
    _, pull_gelu = jax.vjp(jax.nn.gelu, inner)
    (grad_inner,) = pull_gelu(grad_cond)
    grad_normed = jnp.dot(grad_inner, mats[:, FOUR : FOUR + CD].T, precision=HIGH)
    _, pull_norm = jax.vjp(rms_norm, cond_zero)
    (grad_zero,) = pull_norm(grad_normed)
    return (grad_zero + grad_cond, grad_inner)


def scale_norm(hidden, scale):
    return rms_norm(hidden) * scale[:, None, :]


def norm_back(hidden, scale, grad):
    _, pull = jax.vjp(scale_norm, hidden, scale)
    return pull(grad)


class Links:
    def __init__(self, size):
        self.size = size
        self.bits = size.bit_length() - 1
        assert 1 << self.bits == size
        self.upper = list(range(self.bits - 1, 1, -1))

    def flip(self, value, bit):
        return lax.ppermute(value, "dp", [(i, i ^ (1 << bit)) for i in range(self.size)])

    def flip_pair(self, value):
        return lax.ppermute(value, "tensor", [(0, 1), (1, 0)])

    def grow(self, value, bit, axis=0):
        return jnp.concatenate([value, self.flip(value, bit)], axis=axis)

    def grow_pair(self, value, axis):
        return jnp.concatenate([value, self.flip_pair(value)], axis=axis)

    def gather_pair_last(self, value):
        for bit in self.upper + [1]:
            value = self.grow(value, bit)
        other = self.flip_pair(value)
        return (self.grow(value, 0), self.grow(other, 0))

    def gather_pair_first(self, value, axis):
        for bit in self.upper:
            value = self.grow(value, bit)
        value = self.grow_pair(value, axis)
        return self.grow(self.grow(value, 1), 0)

    def halve(self, value, bit):
        half = value.shape[0] // 2
        return value[:half] + self.flip(value[half:], bit)

    def halve_pair(self, value, axis):
        half = value.shape[axis] // 2
        own = lax.slice_in_dim(value, 0, half, axis=axis)
        other = lax.slice_in_dim(value, half, 2 * half, axis=axis)
        return own + self.flip_pair(other)

    def reduce(self, own, other, axis, pair_first):
        value = own + self.flip(other, 0)
        if pair_first:
            value = self.halve(self.halve_pair(value, axis), 1)
        else:
            value = self.halve_pair(self.halve(value, 1), axis)
        for bit in reversed(self.upper):
            value = self.halve(value, bit)
        return value

    def gather_rows(self, value):
        for bit in self.upper + [1]:
            value = self.grow(value, bit)
        return self.grow(self.grow_pair(value, 0), 0)

    def total(self, value):
        value = value + self.flip(value, 0)
        value = value + self.flip_pair(value)
        for bit in [1] + self.upper[::-1]:
            value = value + self.flip(value, bit)
        return value


def reverse_bits(value, bits):
    result = 0
    for bit in range(bits):
        result |= ((value >> bit) & 1) << (bits - 1 - bit)
    return result


def relative_order(size, bits, own):
    block = size >> bits
    order = jnp.array([reverse_bits(i, bits) for i in range(1 << bits)], jnp.int32)
    return ((order ^ own)[:, None] * block + jnp.arange(block)[None, :]).reshape(-1)


def order_matrix(size, order):
    return jnp.arange(size)[:, None] == order[None, :]


def split_heads(project):
    images, tokens = (project.shape[0], project.shape[1])
    return tuple(
        (project[:, :, :, part].reshape(images, tokens, -1, HEAD_DIM) for part in range(3))
    )


def attention_probs(queries, keys, totals):
    scores = einsum_low("iqhe,ikhe->ihqk", queries, keys) * (1.0 / math.sqrt(HEAD_DIM))
    return jnp.exp(scores - totals)


def body(
    clean_images,
    noise_draw,
    levels,
    labels,
    dropped,
    groups,
    step_count,
    inward,
    first_inward,
    second_inward,
    outward,
    first_outward,
    second_outward,
    expand,
    first_expand,
    second_expand,
    shrink,
    first_shrink,
    second_shrink,
    patches,
    first_patches,
    second_patches,
    classes,
    first_classes,
    second_classes,
    mapping,
    first_mapping,
    second_mapping,
):
    masters = (inward, outward, expand, shrink, patches, classes, mapping)
    firsts = (
        first_inward,
        first_outward,
        first_expand,
        first_shrink,
        first_patches,
        first_classes,
        first_mapping,
    )
    seconds = (
        second_inward,
        second_outward,
        second_expand,
        second_shrink,
        second_patches,
        second_classes,
        second_mapping,
    )
    links = Links(lax.axis_size("dp"))
    me, pair = lax.axis_index("dp"), lax.axis_index("tensor")
    images = clean_images.shape[0]
    rows = images * SEQ
    heads_width = inward.shape[2]
    ff_width = expand.shape[2]

    all_axes = ("dp", "tensor")
    table = lax.all_gather(classes.astype(LOW), all_axes, axis=1, tiled=True)
    map_mats = lax.all_gather(mapping.astype(LOW), all_axes, axis=0, tiled=True)
    patch_rows = patches.shape[1]
    patch_flat = jnp.concatenate([patches[0], patches[1]], axis=1).astype(LOW)
    patch_all = links.gather_pair_first(patch_flat, 0)
    attn_in = links.gather_pair_first(inward.reshape(inward.shape[0], -1).astype(LOW), 1)
    attn_out = links.gather_pair_last(outward.T.astype(LOW))
    gate_up = links.gather_pair_last(expand.reshape(expand.shape[0], -1).astype(LOW))
    down = links.gather_pair_first(shrink.T.astype(LOW), 1)

    order_d = relative_order(D, links.bits, me)
    to_own = order_matrix(D, order_d).astype(LOW)
    n_up = len(links.upper)
    pos = []
    for i in range(1 << (links.bits + 1)):
        place, bit = 0, 0
        for step in links.upper:
            place |= ((i >> bit) & 1) << (step + 1)
            bit += 1
        place |= ((i >> bit) & 1) << 0
        place |= ((i >> (bit + 1)) & 1) << 2
        place |= ((i >> (bit + 2)) & 1) << 1
        pos.append(place)
    own_place = me * 2 + pair
    order_p = (
        (jnp.array(pos, jnp.int32) ^ own_place)[:, None] * patch_rows + jnp.arange(patch_rows)[None, :]
    ).reshape(-1)
    to_own_p = order_matrix(PD, order_p).astype(LOW)

    def pick_p(value):
        return jnp.dot(
            value.reshape(rows, PD), to_own_p, preferred_element_type=jnp.float32
        ).reshape(value.shape)

    sigma, radius, feats = noise_terms(levels)
    chosen = jnp.where(dropped == 1, CLASSES - 1, labels)
    onehot = (chosen[:, None] == jnp.arange(CLASSES)[None, :]).astype(jnp.float32)
    map_mats = map_mats.astype(jnp.float32)
    scale_flat, map_kept = map_forward(feats, onehot, table.astype(jnp.float32), map_mats)
    feats_low, cond_zero, normed, inner, cond_low = map_kept
    scales = jnp.dot(
        scale_flat.reshape(images * 3, D), to_own.astype(jnp.float32), precision=HIGH
    ).reshape(images, 3, D)

    sig = sigma[:, None, None]
    rad = radius[:, None, None]
    clean_float = pick_p(clean_images)
    noise_float = pick_p(noise_draw)
    inputs = ((clean_float + sig * noise_float) / rad).astype(LOW)
    target = (sig * clean_float - SIGMA_DATA * SIGMA_DATA * noise_float) / (SIGMA_DATA * rad)

    patch_in = jnp.dot(patch_all[:, :D], to_own, preferred_element_type=jnp.float32).astype(LOW)
    patch_out = jnp.dot(patch_all[:, D:], to_own, preferred_element_type=jnp.float32).astype(LOW)

    resid_zero = einsum_low("isp,pd->isd", inputs, patch_in)
    rows_zero = scale_norm(resid_zero, scales[:, 0]).astype(LOW)
    project = einsum_low("isd,dn->isn", rows_zero, attn_in).astype(LOW)
    project = project.reshape(images, SEQ, 2, 3, heads_width)
    queries, keys, values = split_heads(project)
    scores = einsum_low("iqhe,ikhe->ihqk", queries, keys) * (1.0 / math.sqrt(HEAD_DIM))
    totals = jax.nn.logsumexp(scores, axis=-1, keepdims=True)
    probs = jnp.exp(scores - totals).astype(LOW)
    mixed = einsum_low("ihqk,ikhe->iqhe", probs, values).astype(LOW)
    mixed = mixed.reshape(images, SEQ, -1)
    halves = (mixed[:, :, :heads_width], mixed[:, :, heads_width:])
    resid_one = (
        resid_zero
        + einsum_low("ish,dh->isd", halves[0], attn_out[0])
        + einsum_low("ish,dh->isd", halves[1], attn_out[1])
    )
    rows_one = scale_norm(resid_one, scales[:, 1]).astype(LOW)
    gates, uppers, hiddens = [], [], []
    for part in range(2):
        gates.append(einsum_low("isd,df->isf", rows_one, gate_up[part][:, :ff_width]))
        uppers.append(einsum_low("isd,df->isf", rows_one, gate_up[part][:, ff_width:]))
        hiddens.append((jax.nn.gelu(gates[part]) * uppers[part]).astype(LOW))
    hidden = jnp.concatenate(hiddens, axis=2)
    resid_two = resid_one + einsum_low("isf,df->isd", hidden, down)
    last = scale_norm(resid_two, scales[:, 2]).astype(LOW)
    output = einsum_low("isd,pd->isp", last, patch_out)

    counts = jnp.sum((groups[:, None] == groups[None, :]).astype(jnp.float32), axis=1)
    weight = 1.0 / (GROUPS * counts)
    diff = output - target
    local_loss = jnp.sum(weight * jnp.mean(diff**2, axis=(1, 2)))
    grad_low = (2.0 * diff * (weight / (SEQ * PD))[:, None, None]).astype(LOW)

    half = D // 2

    def weight_grad(form, left, right):
        return einsum_low(form, left, right).astype(LOW)

    grad_last = einsum_low("isp,pd->isd", grad_low, patch_out)
    last_canon = einsum_low("isd,cd->isc", last, to_own).astype(LOW)
    half_p = PD // 2
    out_own = weight_grad("isp,isd->pd", grad_low[:, :, :half_p], last_canon)
    out_other = weight_grad("isp,isd->pd", grad_low[:, :, half_p:], last_canon)
    grad_two, scale_two = norm_back(resid_two, scales[:, 2], grad_last)
    rows_grad = grad_two.astype(LOW)
    grad_hidden = einsum_low("isd,df->isf", rows_grad, down)
    down_own = weight_grad("isd,isf->df", rows_grad[:, :, :half], hidden)
    down_other = weight_grad("isd,isf->df", rows_grad[:, :, half:], hidden)
    shard_down = links.reduce(down_own, down_other, 1, False)

    part_one = 0.0
    gated_grads = []
    for part in range(2):
        _, pull_gate = jax.vjp(
            lambda gate, upper: jax.nn.gelu(gate) * upper, gates[part], uppers[part]
        )
        grad_gate, grad_up = pull_gate(
            grad_hidden[:, :, part * ff_width : (part + 1) * ff_width]
        )
        gated_grads.append(jnp.concatenate([grad_gate, grad_up], axis=2).astype(LOW))
        part_one = part_one + einsum_low("isf,df->isd", gated_grads[part], gate_up[part])
    gated_grad = jnp.concatenate(gated_grads, axis=2)
    up_own = weight_grad("isd,isf->df", rows_one[:, :, :half], gated_grad)
    up_other = weight_grad("isd,isf->df", rows_one[:, :, half:], gated_grad)
    shard_up = links.reduce(up_own, up_other, 1, True)

    part_one, scale_one = norm_back(resid_one, scales[:, 1], part_one)
    grad_one = grad_two + part_one
    rows_grad = grad_one.astype(LOW)
    grad_mixed = jnp.concatenate(
        [
            einsum_low("isd,dh->ish", rows_grad, attn_out[0]),
            einsum_low("isd,dh->ish", rows_grad, attn_out[1]),
        ],
        axis=2,
    ).astype(LOW)
    attn_own = weight_grad("isd,ish->dh", rows_grad[:, :, :half], mixed)
    attn_other = weight_grad("isd,ish->dh", rows_grad[:, :, half:], mixed)
    shard_out = links.reduce(attn_own, attn_other, 1, True)
    grad_mixed = grad_mixed.reshape(queries.shape)

    probs = attention_probs(queries, keys, totals)
    grad_values = einsum_low("ihqk,iqhe->ikhe", probs.astype(LOW), grad_mixed)
    grad_probs = einsum_low("iqhe,ikhe->ihqk", grad_mixed, values)
    grad_scores = (
        probs * (grad_probs - jnp.sum(grad_probs * probs, axis=-1, keepdims=True))
    ).astype(LOW)
    inverse_root = 1.0 / math.sqrt(HEAD_DIM)
    grad_queries = einsum_low("ihqk,ikhe->iqhe", grad_scores, keys) * inverse_root
    grad_keys = einsum_low("ihqk,iqhe->ikhe", grad_scores, queries) * inverse_root
    grad_project = jnp.stack(
        [
            part.reshape(images, SEQ, 2, heads_width).astype(LOW)
            for part in (grad_queries, grad_keys, grad_values)
        ],
        axis=3,
    ).reshape(images, SEQ, -1)
    in_own = weight_grad("isd,isn->dn", rows_zero[:, :, :half], grad_project)
    in_other = weight_grad("isd,isn->dn", rows_zero[:, :, half:], grad_project)
    shard_in = links.reduce(in_own, in_other, 1, False)

    part_zero, scale_zero = norm_back(
        resid_zero, scales[:, 0], einsum_low("isn,dn->isd", grad_project, attn_in)
    )
    grad_zero = (grad_one + part_zero).astype(LOW)
    zero_canon = einsum_low("isd,cd->isc", grad_zero, to_own).astype(LOW)
    patch_own = jnp.concatenate(
        [weight_grad("isp,isd->pd", inputs[:, :, :half_p], zero_canon), out_own], axis=1
    )
    patch_other = jnp.concatenate(
        [weight_grad("isp,isd->pd", inputs[:, :, half_p:], zero_canon), out_other], axis=1
    )
    shard_patch = links.reduce(patch_own, patch_other, 0, False)

    grad_scales = jnp.stack([scale_zero, scale_one, scale_two], axis=1)
    grad_scales = jnp.dot(
        grad_scales.reshape(images * 3, D), to_own.astype(jnp.float32).T, precision=HIGH
    ).reshape(images, 3 * D)
    map_grad_zero, map_grad_inner = map_backward(map_mats, map_kept, grad_scales)
    kept_rows = jnp.concatenate([feats_low, normed, cond_low], axis=1).astype(LOW)
    kept_rows = links.gather_rows(kept_rows).astype(jnp.float32)
    chosen_rows = links.gather_rows(jnp.broadcast_to(chosen[:, None], (images, 128)))[:, :1]
    grad_rows = links.gather_rows(
        jnp.concatenate([grad_scales, map_grad_inner, map_grad_zero], axis=1)
    )
    own = own_place * mapping.shape[0]

    def own_columns(value):
        return lax.dynamic_slice_in_dim(value, own, mapping.shape[0], axis=1)

    zero_own = own_columns(grad_rows[:, 3 * D + CD :])
    onehot_rows = (chosen_rows == jnp.arange(CLASSES)[None, :]).astype(jnp.float32)
    table_grad = outer_sum(onehot_rows, zero_own)
    mapping_grad = jnp.concatenate(
        [
            outer_sum(zero_own, kept_rows[:, :FOUR]),
            outer_sum(own_columns(kept_rows[:, FOUR : FOUR + CD]), grad_rows[:, 3 * D : 3 * D + CD]),
            outer_sum(own_columns(kept_rows[:, FOUR + CD :]), grad_rows[:, : 3 * D]),
        ],
        axis=1,
    )

    shard_patch = shard_patch.astype(jnp.float32)
    grads = (
        shard_in.astype(jnp.float32).reshape(inward.shape),
        shard_out.astype(jnp.float32).T,
        shard_up.astype(jnp.float32).reshape(expand.shape),
        shard_down.astype(jnp.float32).T,
        jnp.stack([shard_patch[:, :D], shard_patch[:, D:]]),
        table_grad,
        mapping_grad,
    )
    squares = sum((jnp.sum(grad * grad) for grad in grads))
    sums = links.total(jnp.stack([local_loss, squares]))
    total_loss = sums[0]
    grad_norm = jnp.sqrt(sums[1])
    factor = CLIP / (grad_norm + NORM_EPS)
    count = step_count[0].astype(jnp.float32)
    fix_one = 1.0 - jnp.power(BETA_ONE, count)
    fix_two = 1.0 - jnp.power(BETA_TWO, count)
    results = [total_loss, grad_norm]
    for master, first, second, grad in zip(masters, firsts, seconds, grads):
        clipped = grad * factor
        moment = BETA_ONE * first + (1.0 - BETA_ONE) * clipped
        square = BETA_TWO * second + (1.0 - BETA_TWO) * clipped * clipped
        step_size = moment / fix_one / (jnp.sqrt(square / fix_two) + ADAM_EPS)
        results.extend([master - LEARN_RATE * (step_size + DECAY * master), moment, square])
    return tuple(results)


def solution(mesh):
    in_specs = (
        P(("dp", "tensor"), None, None),
        P(("dp", "tensor"), None, None),
        P(("dp", "tensor")),
        P(("dp", "tensor")),
        P(("dp", "tensor")),
        P(("dp", "tensor")),
        P(),
        P("dp", None, "tensor"),
        P("dp", None, "tensor"),
        P("dp", None, "tensor"),
        P("tensor", "dp"),
        P("tensor", "dp"),
        P("tensor", "dp"),
        P("dp", None, "tensor"),
        P("dp", None, "tensor"),
        P("dp", None, "tensor"),
        P("tensor", "dp"),
        P("tensor", "dp"),
        P("tensor", "dp"),
        P(None, ("dp", "tensor"), None),
        P(None, ("dp", "tensor"), None),
        P(None, ("dp", "tensor"), None),
        P(None, ("dp", "tensor")),
        P(None, ("dp", "tensor")),
        P(None, ("dp", "tensor")),
        P(("dp", "tensor"), None),
        P(("dp", "tensor"), None),
        P(("dp", "tensor"), None),
    )
    out_specs = (
        P(),
        P(),
        P("dp", None, "tensor"),
        P("dp", None, "tensor"),
        P("dp", None, "tensor"),
        P("tensor", "dp"),
        P("tensor", "dp"),
        P("tensor", "dp"),
        P("dp", None, "tensor"),
        P("dp", None, "tensor"),
        P("dp", None, "tensor"),
        P("tensor", "dp"),
        P("tensor", "dp"),
        P("tensor", "dp"),
        P(None, ("dp", "tensor"), None),
        P(None, ("dp", "tensor"), None),
        P(None, ("dp", "tensor"), None),
        P(None, ("dp", "tensor")),
        P(None, ("dp", "tensor")),
        P(None, ("dp", "tensor")),
        P(("dp", "tensor"), None),
        P(("dp", "tensor"), None),
        P(("dp", "tensor"), None),
    )
    return jax.shard_map(body, mesh=mesh, in_specs=in_specs, out_specs=out_specs, check_vma=False)
```

```python
import math
import types

import jax
import jax.numpy as jnp
from jax import lax
from jax.experimental import pallas as pl
from jax.experimental.pallas import tpu as pltpu
from jax.sharding import PartitionSpec as P

D = 1024
HEAD_DIM = 64
CD = 768
CLASSES = 1001
PD = 768
FOUR = 256
SEQ = 256
GROUPS = 4
NLEVELS = 1000
LOW = jnp.bfloat16
F32 = jnp.float32
TILE = 512
TABLE = 1024


HIGH = lax.Precision.HIGHEST
SIGMA_DATA = 0.5
LEARN_RATE = 0.05
DECAY = 0.1
BETA_ONE = 0.5
BETA_TWO = 0.5
ADAM_EPS = 1e-08
CLIP = 0.02
NORM_EPS = 1e-06
MIB = 1 << 20


def rms_norm(value):
    return value * lax.rsqrt(jnp.mean(value * value, axis=-1, keepdims=True) + NORM_EPS)


def dot_f32(left, right):
    return jnp.dot(left, right, preferred_element_type=F32)


def dot_nt(left, right):
    return lax.dot_general(left, right, (((1,), (1,)), ((), ())), preferred_element_type=F32)


def dot_tn(left, right):
    return lax.dot_general(left, right, (((0,), (0,)), ((), ())), preferred_element_type=F32)


def noise_terms(levels):
    log_sigma = -3.0 + 6.0 * levels.astype(F32) / (NLEVELS - 1)
    sigma = jnp.exp(log_sigma)
    radius = jnp.sqrt(sigma * sigma + SIGMA_DATA * SIGMA_DATA)
    half = FOUR // 2
    freqs = jnp.exp(-2.0 + 4.0 * jnp.arange(half, dtype=F32) / (half - 1))
    angles = 2.0 * math.pi * (log_sigma / 4.0)[:, None] * freqs[None, :]
    return (sigma, radius, jnp.concatenate([jnp.cos(angles), jnp.sin(angles)], axis=1))


class Rounds:
    def __init__(self, have):
        self.token = jnp.zeros((8, 128), F32)
        self.have, self.tied = have, set()

    def __call__(self, runs, works, held=()):
        fields = {name: value for name, value in vars(self.have).items() if name not in self.tied}
        values, form = jax.tree.flatten((fields, [run.waiting for run in (*runs, *held)]))
        *values, self.token = lax.optimization_barrier((*values, self.token))
        fields, waiting = jax.tree.unflatten(form, values)
        vars(self.have).update(fields)
        self.tied.update(fields)
        for run, value in zip(held, waiting[len(runs) :]):
            run.waiting = value
        for run, value in zip(runs, waiting):
            run.go_on(value)
        for work in works:
            work()


def params(vmem=40):
    return pltpu.CompilerParams(vmem_limit_bytes=vmem * MIB)


def cost(*_):
    return pl.CostEstimate(flops=1, bytes_accessed=1, transcendentals=0)


def simple(kernel, columns, in_specs, args, out_rows, out_lead=()):
    width = columns
    while width > 1024 and width % 256 == 0:
        width //= 2
    return pl.pallas_call(
        kernel,
        grid=(columns // width,),
        in_specs=[spec(width) for spec in in_specs],
        out_specs=[pl.BlockSpec((rows, width), lambda j: (0, j)) for rows in out_rows],
        out_shape=[jax.ShapeDtypeStruct((rows, columns), LOW) for rows in out_rows],
        compiler_params=params(),
        cost_estimate=cost(),
    )(*args)


def rows_spec(rows, at=0):
    return lambda width: pl.BlockSpec((rows, width), lambda j: (at, j))


def part_spec(pair, half, at):
    return lambda width: pl.BlockSpec((1, half, width), lambda j: (pair, at, j))


def even(*rows):
    return all(row % 16 == 0 for row in rows)


def one_below_other(*parts):
    rows, columns = parts[0].shape
    if not even(rows):
        return jnp.concatenate(parts, axis=0)

    def kernel(*refs):
        *refs, out_ref = refs
        for i, ref in enumerate(refs):
            out_ref[i * rows : (i + 1) * rows, :] = ref[...]

    specs = [rows_spec(rows)] * len(parts)
    return simple(kernel, columns, specs, parts, (len(parts) * rows,))[0]


def top_and_bottom(first, second):
    rows, columns = first.shape
    half = rows // 2
    if not even(half):
        return first[:half], second[half:]

    def kernel(first_ref, second_ref, top_ref, bottom_ref):
        top_ref[...] = first_ref[...]
        bottom_ref[...] = second_ref[...]

    specs = [rows_spec(half), rows_spec(half, 1)]
    return simple(kernel, columns, specs, (first, second), (half, half))


def add(*terms):
    return sum(term.astype(F32) for term in terms).astype(LOW)


def add_corners(own, came):
    _, rows, columns = own.shape
    half = rows // 2
    quarter = half // 2
    if not even(quarter):
        total = add(own[1, half:], came)
        return total[:quarter], total[quarter:]

    def kernel(own_ref, came_ref, x_ref, pair_ref):
        x_ref[...] = add(own_ref[0, :quarter], came_ref[:quarter])
        pair_ref[...] = add(own_ref[0, quarter:], came_ref[quarter:])

    specs = [part_spec(1, half, 1), rows_spec(half)]
    return simple(kernel, columns, specs, (own, came), (quarter, quarter))


def add_sides(own, came_pair, came_x, from_x, from_pair):
    _, rows, columns = own.shape
    half = rows // 2
    quarter = half // 2
    if not even(quarter):
        to_pair = add(own[1, :half], came_pair, jnp.pad(from_x, ((0, half - quarter), (0, 0))))
        to_x = add(own[0, half:], came_x, jnp.pad(from_pair, ((quarter, 0), (0, 0))))
        return to_pair, to_x

    def kernel(own_a, came_a, own_b, came_b, x_ref, pair_ref, to_pair, to_x):
        to_pair[:quarter, :] = add(own_a[0, :quarter], came_a[:quarter], x_ref[...])
        to_pair[quarter:, :] = add(own_a[0, quarter:], came_a[quarter:])
        to_x[:quarter, :] = add(own_b[0, :quarter], came_b[:quarter])
        to_x[quarter:, :] = add(own_b[0, quarter:], came_b[quarter:], pair_ref[...])

    first, second = part_spec(1, half, 0), part_spec(0, half, 1)
    side, corner = rows_spec(half), rows_spec(quarter)
    specs = [first, side, second, side, corner, corner]
    args = (own, came_pair, own, came_x, from_x, from_pair)
    return simple(kernel, columns, specs, args, (half, half))


def add_parts(count, *terms):
    columns = terms[0].shape[-1]
    rows = terms[-1].shape[0]
    size = rows // count
    cuts = [slice(i * size, (i + 1) * size) for i in range(count)]
    if not even(size):
        terms = [term[0, :rows] if term.ndim == 3 else term for term in terms]
        return tuple(add(*(term[cut] for term in terms)) for cut in cuts)

    def kernel(*refs):
        refs, outs = refs[: len(terms)], refs[len(terms) :]
        parts = [ref.at[0] if len(ref.shape) == 3 else ref for ref in refs]
        for cut, out in zip(cuts, outs):
            out[...] = add(*(part[cut, :] for part in parts))

    specs = [part_spec(0, rows, 0) if term.ndim == 3 else rows_spec(rows) for term in terms]
    return simple(kernel, columns, specs, terms, (size,) * count)


class Links:
    def __init__(self, size):
        self.size = size
        self.bits = size.bit_length() - 1
        assert 1 << self.bits == size
        self.upper = list(range(self.bits - 1, 1, -1))

    def swap(self, value, mask):
        return lax.ppermute(value, "dp", [(i, i ^ mask) for i in range(self.size)])

    def flip(self, value, bit):
        return self.swap(value, 1 << bit)

    def far(self):
        if len(self.upper) != 2:
            return None
        first, second = (1 << bit for bit in self.upper)
        return (first, second, first | second)

    def flip_pair(self, value):
        return lax.ppermute(value, "tensor", [(0, 1), (1, 0)])

    def gather(self, value, groups=((0, 1, 2),)):
        if self.far():
            (value,) = yield (value,)
            parts = [value]
            for group in groups:
                parts = [*parts] + [self.swap(value, self.far()[i]) for i in group]
                parts = yield tuple(parts)
            value = one_below_other(*parts)
        else:
            for bit in self.upper:
                (value,) = yield (value,)
                value = one_below_other(value, self.flip(value, bit))
            (value,) = yield (value,)
        by_x, by_pair = self.flip(value, 1), self.flip_pair(value)
        by_x, by_pair = yield (by_x, by_pair)
        top, bottom = top_and_bottom(by_pair, by_x)
        corner = (self.flip(top, 1), self.flip_pair(bottom))
        pieces = [value, by_x, by_pair, *corner]
        pieces = yield tuple(pieces)
        pieces = list(pieces)
        return pieces + [self.flip(piece, 0) for piece in pieces]

    def gather_rows(self, value):
        for bit in (1, None, 0):
            (value,) = yield (value,)
            other = self.flip_pair(value) if bit is None else self.flip(value, bit)
            value = jnp.concatenate([value, other], axis=0)
        return value


    def place(self, index):
        return sum(((index >> i) & 1) << (bit - 2) for i, bit in enumerate(self.upper))

    def index(self, place):
        return sum(((place >> (bit - 2)) & 1) << i for i, bit in enumerate(self.upper))

    def along(self, values):
        others = [
            self.swap(value, self.place(i + 1) << 2) for i, value in enumerate(values[1:])
        ]
        return [values[0], *others]

    def seen_from_here(self, value, index):
        order = [i ^ index for i in range(value.shape[0])]
        return jnp.concatenate([value[i : i + 1] for i in order], axis=0)

    def reduce(self, own, *others):
        others = yield others
        corner, side, across, kept = (self.flip(others[i], 0) for i in (3, 2, 1, 0))
        (corner,) = yield (corner,)
        corner_x, corner_pair = add_corners(own, corner)
        from_x, from_pair = self.flip(corner_x, 1), self.flip_pair(corner_pair)
        from_x, from_pair, side, across = yield (from_x, from_pair, side, across)
        to_pair, to_x = add_sides(own, side, across, from_x, from_pair)
        came = kept
        terms = (own, came, self.flip_pair(to_pair), self.flip(to_x, 1))
        if self.far():
            terms = yield terms
            kept, *sent = add_parts(4, *terms)
            terms = (kept, *(self.swap(part, mask) for part, mask in zip(sent, self.far())))
        else:
            for bit in reversed(self.upper):
                terms = yield terms
                kept, sent = add_parts(2, *terms)
                terms = (kept, self.flip(sent, bit))
        terms = yield terms
        return sum(term.astype(F32) for term in terms)

    def total(self, value):
        value = value + self.flip(value, 0)
        value = value + self.flip_pair(value)
        for bit in [1] + self.upper[::-1]:
            value = value + self.flip(value, bit)
        return value


class Run:
    def __init__(self, steps=None):
        self.result = None
        if steps is not None:
            self.begin(steps)

    def begin(self, steps):
        self.steps, self.waiting = steps, next(steps)

    def go_on(self, values):
        assert self.result is None
        try:
            self.waiting = self.steps.send(values)
        except StopIteration as stop:
            self.result = stop.value

    def finish(self):
        while self.result is None:
            self.go_on(self.waiting)
        return self.result


def reverse_bits(value, bits):
    result = 0
    for bit in range(bits):
        result |= ((value >> bit) & 1) << (bits - 1 - bit)
    return result


def spread(places, own, block):
    order = jnp.array(places, jnp.int32) ^ own
    return (order[:, None] * block + jnp.arange(block)[None, :]).reshape(-1)


def order_matrix(size, order):
    return (jnp.arange(size)[:, None] == order[None, :]).astype(LOW)


def whole(shape):
    return pl.BlockSpec(shape, lambda *_: (0,) * len(shape))


def piece_specs(pieces, width, at):
    return [pl.BlockSpec((piece.shape[0], width), lambda j: (0, at + j)) for piece in pieces]


def both_spec(rows, width, at=0):
    return pl.BlockSpec((2, rows, width), lambda j: (0, 0, at + j))


def assemble(pieces):
    starts = [0]
    for piece in pieces:
        starts.append(starts[-1] + piece.shape[0])
    columns = pieces[0].shape[1]

    def kernel(*refs):
        *refs, out_ref = refs
        for ref, start in zip(refs, starts):
            out_ref[start : start + ref.shape[0], :] = ref[...]

    return pl.pallas_call(
        kernel,
        grid=(columns // (2 * TILE),),
        in_specs=piece_specs(pieces, 2 * TILE, 0),
        out_specs=pl.BlockSpec((starts[-1], 2 * TILE), lambda j: (0, j)),
        out_shape=jax.ShapeDtypeStruct((starts[-1], columns), LOW),
        compiler_params=params(),
        cost_estimate=cost(),
    )(*pieces)


def rows_matmul(x, matrix, columns, at):
    rows = x.shape[0]

    def kernel(x_ref, matrix_ref, out_ref):
        for pair in range(2):
            out_ref[pair] = dot_f32(x_ref[...], matrix_ref[pair]).astype(LOW)

    return pl.pallas_call(
        kernel,
        grid=(columns // TILE,),
        in_specs=[whole(x.shape), both_spec(D, TILE, at)],
        out_specs=both_spec(rows, TILE),
        out_shape=jax.ShapeDtypeStruct((2, rows, columns), LOW),
        compiler_params=params(),
        cost_estimate=cost(),
    )(x, matrix)


def expand_forward(x, matrix, columns):
    rows = x.shape[0]

    def kernel(x_ref, matrix_ref, gated_ref, hidden_ref):
        for pair in range(2):
            gate = dot_f32(x_ref[...], matrix_ref[pair, :, :TILE])
            upper = dot_f32(x_ref[...], matrix_ref[pair, :, TILE:])
            gated_ref[pair, :, :TILE] = gate.astype(LOW)
            gated_ref[pair, :, TILE:] = upper.astype(LOW)
            hidden_ref[pair] = (jax.nn.gelu(gate) * upper).astype(LOW)

    return pl.pallas_call(
        kernel,
        grid=(columns // (2 * TILE),),
        in_specs=[whole(x.shape), both_spec(D, 2 * TILE)],
        out_specs=[both_spec(rows, 2 * TILE), both_spec(rows, TILE)],
        out_shape=[
            jax.ShapeDtypeStruct((2, rows, columns), LOW),
            jax.ShapeDtypeStruct((2, rows, columns // 2), LOW),
        ],
        compiler_params=params(),
        cost_estimate=cost(),
    )(x, matrix)


def gelu_parts(gate):
    root, cube = math.sqrt(2.0 / math.pi), 0.044715
    square = gate * gate
    slope = jnp.tanh(root * (gate + cube * gate * square))
    half = 0.5 * (1.0 + slope)
    turn = 0.5 * gate * (1.0 - slope * slope) * root * (1.0 + 3.0 * cube * square)
    return gate * half, half + turn


def shrink_backward(x, matrix, at, gated):
    rows = x.shape[0]
    columns = gated.shape[2] // 2

    def kernel(x_ref, gated_ref, matrix_ref, out_ref):
        for pair in range(2):
            grad = dot_f32(x_ref[...], matrix_ref[pair])
            gate = gated_ref[pair, :, :TILE].astype(F32)
            upper = gated_ref[pair, :, TILE:].astype(F32)
            value, slope = gelu_parts(gate)
            out_ref[pair, :, :TILE] = (grad * upper * slope).astype(LOW)
            out_ref[pair, :, TILE:] = (grad * value).astype(LOW)

    both = both_spec(rows, 2 * TILE)
    return pl.pallas_call(
        kernel,
        grid=(columns // TILE,),
        in_specs=[whole(x.shape), both, both_spec(D, TILE, at)],
        out_specs=both,
        out_shape=jax.ShapeDtypeStruct(gated.shape, LOW),
        compiler_params=params(),
        cost_estimate=cost(),
    )(x, gated, matrix)


def cols_sum(value_ref, matrix_ref):
    return dot_nt(value_ref[0], matrix_ref[0]) + dot_nt(value_ref[1], matrix_ref[1])


def norm_out(value, scale_ref, resid_ref, rows_ref):
    images = scale_ref.shape[0]
    resid_ref[...] = value
    for i in range(images):
        span = slice(i * SEQ, (i + 1) * SEQ)
        part = resid_ref[span, :]
        rows_ref[span, :] = (rms_norm(part) * scale_ref[i : i + 1, :]).astype(LOW)


def norm_grad(resid, scale, grad):
    root = lax.rsqrt(jnp.mean(resid * resid, axis=-1, keepdims=True) + NORM_EPS)
    normed = resid * root
    inner = grad * scale
    back = root * (inner - normed * jnp.mean(inner * normed, axis=-1, keepdims=True))
    return back, jnp.sum(grad * normed, axis=0, keepdims=True)


def cols_forward(value, matrix, width, at, resid, scale):
    _, rows, columns = value.shape
    steps = columns // width

    def kernel(value_ref, resid_ref, scale_ref, matrix_ref, out_ref, rows_ref, acc_ref):
        @pl.when(pl.program_id(0) == 0)
        def _():
            acc_ref[...] = resid_ref[...]

        acc_ref[...] += cols_sum(value_ref, matrix_ref)

        @pl.when(pl.program_id(0) == steps - 1)
        def _():
            norm_out(acc_ref[...], scale_ref, out_ref, rows_ref)

    return pl.pallas_call(
        kernel,
        grid=(steps,),
        in_specs=[
            both_spec(rows, width),
            whole(resid.shape),
            whole(scale.shape),
            both_spec(D, width, at),
        ],
        out_specs=[whole(resid.shape), whole(resid.shape)],
        out_shape=[
            jax.ShapeDtypeStruct(resid.shape, F32),
            jax.ShapeDtypeStruct(resid.shape, LOW),
        ],
        scratch_shapes=[pltpu.VMEM(resid.shape, F32)],
        compiler_params=params(),
        cost_estimate=cost(),
    )(value, resid, scale, matrix)


def cols_backward(value, matrix, width, at, resid, scale, grad, types):
    _, rows, columns = value.shape
    steps = columns // width

    def kernel(value_ref, resid_ref, scale_ref, grad_ref, matrix_ref, scale_out, *outs):
        *outs, acc_ref = outs

        @pl.when(pl.program_id(0) == 0)
        def _():
            acc_ref[...] = cols_sum(value_ref, matrix_ref)

        @pl.when(pl.program_id(0) > 0)
        def _():
            acc_ref[...] += cols_sum(value_ref, matrix_ref)

        @pl.when(pl.program_id(0) == steps - 1)
        def _():
            for i in range(scale_ref.shape[0]):
                span = slice(i * SEQ, (i + 1) * SEQ)
                back, scale_out[i : i + 1, :] = norm_grad(
                    resid_ref[span, :], scale_ref[i : i + 1, :], acc_ref[span, :]
                )
                back = back + grad_ref[span, :]
                for out in outs:
                    out[span, :] = back.astype(out.dtype)

    return pl.pallas_call(
        kernel,
        grid=(steps,),
        in_specs=[
            both_spec(rows, width),
            whole(resid.shape),
            whole(scale.shape),
            whole(resid.shape),
            both_spec(D, width, at),
        ],
        out_specs=[whole(scale.shape)] + [whole(resid.shape)] * len(types),
        out_shape=[jax.ShapeDtypeStruct(scale.shape, F32)]
        + [jax.ShapeDtypeStruct(resid.shape, kind) for kind in types],
        scratch_shapes=[pltpu.VMEM(resid.shape, F32)],
        compiler_params=params(),
        cost_estimate=cost(),
    )(value, resid, scale, grad, matrix)


def weight_grads(from_own, first, *pairs):
    rows, depth = pairs[0][0].shape
    half = depth // 2
    quarter = half // 2
    tiles = [value.shape[2] // TILE for _, value in pairs]
    starts = [sum(tiles[:i]) for i in range(len(tiles))]
    columns = sum(tiles) * TILE

    def kernel(*refs):
        count = len(pairs)
        order_ref, first_ref, *refs = refs
        x_refs, value_refs = refs[:count], refs[count : 2 * count]
        own_ref, *parts = refs[2 * count : 2 * count + 5]
        turned = refs[2 * count + 5 :]
        step = pl.program_id(0)
        for i in range(count):

            @pl.when(step == starts[i])
            def _():
                turned[i][...] = dot_nt(order_ref[...], x_refs[i][...]).astype(LOW)

            @pl.when((step >= starts[i]) & (step < starts[i] + tiles[i]))
            def _():
                for pair in range(2):
                    value = value_refs[i][first_ref[0] ^ pair]
                    own_ref[pair] = dot_f32(turned[i][:half, :], value).astype(LOW)
                    other = dot_f32(turned[i][half:, :], value).astype(LOW)
                    parts[2 * pair][...] = other[:quarter]
                    parts[2 * pair + 1][...] = other[quarter:]

    def value_spec(i):
        return pl.BlockSpec(
            (2, rows, TILE), lambda j: (0, 0, jnp.clip(j - starts[i], 0, tiles[i] - 1))
        )

    return pl.pallas_call(
        kernel,
        grid=(columns // TILE,),
        in_specs=[whole(from_own.shape), pl.BlockSpec(memory_space=pltpu.SMEM)]
        + [whole(x.shape) for x, _ in pairs]
        + [value_spec(i) for i in range(len(pairs))],
        out_specs=[pl.BlockSpec((2, half, TILE), lambda j: (0, 0, j))]
        + [pl.BlockSpec((quarter, TILE), lambda j: (0, j))] * 4,
        out_shape=[jax.ShapeDtypeStruct((2, half, columns), LOW)]
        + [jax.ShapeDtypeStruct((quarter, columns), LOW)] * 4,
        scratch_shapes=[pltpu.VMEM((depth, rows), LOW) for _ in pairs],
        compiler_params=params(),
        cost_estimate=cost(),
    )(from_own, first, *(x for x, _ in pairs), *(value for _, value in pairs))


def head_part(ref, part):
    return ref[0, :, part * HEAD_DIM : (part + 1) * HEAD_DIM]


def softmax_turned(queries, keys):
    scores = dot_nt(keys, queries) * (1.0 / math.sqrt(HEAD_DIM))
    scores = jnp.exp(scores - jnp.max(scores, axis=0, keepdims=True))
    return scores * (1.0 / jnp.sum(scores, axis=0, keepdims=True))


def attention_specs(width):
    return [
        pl.BlockSpec((1, SEQ, width), lambda i, j, part=part: (i, j, part)) for part in range(3)
    ]


def attention_forward(project, width):
    rows = project.shape[1]

    def kernel(q_ref, k_ref, v_ref, out_ref):
        for part in range(width // HEAD_DIM):
            scores = dot_nt(head_part(q_ref, part), head_part(k_ref, part))
            scores = scores * (1.0 / math.sqrt(HEAD_DIM))
            scores = jnp.exp(scores - jnp.max(scores, axis=-1, keepdims=True))
            probs = scores * (1.0 / jnp.sum(scores, axis=-1, keepdims=True))
            mixed = dot_f32(probs.astype(LOW), head_part(v_ref, part))
            out_ref[0, :, part * HEAD_DIM : (part + 1) * HEAD_DIM] = mixed.astype(LOW)

    return pl.pallas_call(
        kernel,
        grid=(2, rows // SEQ),
        in_specs=attention_specs(width),
        out_specs=pl.BlockSpec((1, SEQ, width), lambda i, j: (i, j, 0)),
        out_shape=jax.ShapeDtypeStruct((2, rows, width), LOW),
        compiler_params=params(),
        cost_estimate=cost(8 * rows * SEQ * width, 16 * rows * width),
    )(project, project, project)


def attention_backward(project, grad, width):
    rows = project.shape[1]
    inverse_root = 1.0 / math.sqrt(HEAD_DIM)

    def kernel(q_ref, k_ref, v_ref, grad_ref, out_ref):
        for part in range(width // HEAD_DIM):
            queries, keys = head_part(q_ref, part), head_part(k_ref, part)
            values, grad = head_part(v_ref, part), head_part(grad_ref, part)
            probs = softmax_turned(queries, keys)
            grad_values = dot_f32(probs.astype(LOW), grad)
            grad_probs = dot_nt(values, grad)
            inner = jnp.sum(grad_probs * probs, axis=0, keepdims=True)
            grad_scores = (probs * (grad_probs - inner)).astype(LOW)
            grad_queries = dot_tn(keys, grad_scores).T * inverse_root
            grad_keys = dot_f32(grad_scores, queries) * inverse_root
            for place, value in enumerate((grad_queries, grad_keys, grad_values)):
                start = place * width + part * HEAD_DIM
                out_ref[0, :, start : start + HEAD_DIM] = value.astype(LOW)

    return pl.pallas_call(
        kernel,
        grid=(2, rows // SEQ),
        in_specs=attention_specs(width) + [pl.BlockSpec((1, SEQ, width), lambda i, j: (i, j, 0))],
        out_specs=pl.BlockSpec((1, SEQ, 3 * width), lambda i, j: (i, j, 0)),
        out_shape=jax.ShapeDtypeStruct((2, rows, 3 * width), LOW),
        compiler_params=params(),
        cost_estimate=cost(20 * rows * SEQ * width, 28 * rows * width),
    )(project, project, project, grad)


def loss_kernel(last, patch_out, target, coef, resid, scale):
    rows = last.shape[0]
    images = scale.shape[0]

    def kernel(
        last_ref, out_ref, target_ref, coef_ref, resid_ref, scale_ref,
        loss_ref, low_ref, grad_ref, rows_ref, scale_out,
    ):
        for i in range(images):
            span = slice(i * SEQ, (i + 1) * SEQ)
            diff = dot_nt(last_ref[span, :], out_ref[...]) - target_ref[span, :]
            total = jnp.sum(jnp.sum(diff * diff, axis=1, keepdims=True), axis=0, keepdims=True)
            loss_ref[i : i + 1, :] = jnp.broadcast_to(total, (1, 128))
            low = (diff * coef_ref[i : i + 1, :1]).astype(LOW)
            low_ref[span, :] = low
            back, scale_out[i : i + 1, :] = norm_grad(
                resid_ref[span, :], scale_ref[i : i + 1, :], dot_f32(low, out_ref[...])
            )
            grad_ref[span, :] = back
            rows_ref[span, :] = back.astype(LOW)

    return pl.pallas_call(
        kernel,
        out_shape=[
            jax.ShapeDtypeStruct((images, 128), F32),
            jax.ShapeDtypeStruct((rows, PD), LOW),
            jax.ShapeDtypeStruct((rows, D), F32),
            jax.ShapeDtypeStruct((rows, D), LOW),
            jax.ShapeDtypeStruct((images, D), F32),
        ],
        compiler_params=params(),
        cost_estimate=cost(4 * rows * D * PD, 16 * rows * D),
    )(last, patch_out, target, coef, resid, scale)


def body(
    clean_images,
    noise_draw,
    levels,
    labels,
    dropped,
    groups,
    step_count,
    inward,
    first_inward,
    second_inward,
    outward,
    first_outward,
    second_outward,
    expand,
    first_expand,
    second_expand,
    shrink,
    first_shrink,
    second_shrink,
    patches,
    first_patches,
    second_patches,
    classes,
    first_classes,
    second_classes,
    mapping,
    first_mapping,
    second_mapping,
):
    masters = (inward, outward, expand, shrink, patches, classes, mapping)
    firsts = (
        first_inward,
        first_outward,
        first_expand,
        first_shrink,
        first_patches,
        first_classes,
        first_mapping,
    )
    seconds = (
        second_inward,
        second_outward,
        second_expand,
        second_shrink,
        second_patches,
        second_classes,
        second_mapping,
    )
    links = Links(lax.axis_size("dp"))
    me, pair = lax.axis_index("dp"), lax.axis_index("tensor")
    own_place = me * 2 + pair
    images = clean_images.shape[0]
    rows = images * SEQ
    width = inward.shape[2]
    ff_width = expand.shape[2]
    ff_tiles = ff_width // TILE
    map_rows = mapping.shape[0]

    have = types.SimpleNamespace()
    rounds = Rounds(have)

    def turn(*values):
        return values[0] if len(values) == 1 else values

    flat_patch = jnp.concatenate([patches[0], patches[1]], axis=1).astype(LOW)
    table = jnp.pad(classes.T, ((0, 0), (0, TABLE - CLASSES)))
    flat_map = jnp.concatenate([table, mapping], axis=1).astype(LOW)
    flat_up = expand.reshape(-1, 2, ff_tiles, TILE).transpose(0, 2, 1, 3)
    flat = jnp.concatenate(
        [
            flat_up.reshape(expand.shape[0], -1),
            shrink.T,
            inward.reshape(inward.shape[0], -1),
            outward.T,
        ],
        axis=1,
    ).astype(LOW)
    block = lax.all_gather(flat, ("tensor", "dp"), axis=0, tiled=True)
    block = block.reshape(2, D, flat.shape[1])
    at_down = 2 * ff_tiles
    at_in = 3 * ff_tiles
    at_out = at_in + 3 * width // TILE
    g_p = Run(links.gather(flat_patch))
    g_m = Run(links.gather_rows(flat_map))
    s_p, s_a, s_e, s_s, rows_run = (Run() for _ in range(5))
    line = links.size // 4
    part = 8 * map_rows

    n_up = len(links.upper)

    order_d = spread([reverse_bits(i, links.bits) for i in range(links.size)], me, D // links.size)
    to_own = order_matrix(D, order_d)
    from_own = to_own.T
    this_pair = pair.reshape(1)
    places = []
    for i in range(2 * links.size):
        place = 0
        for bit, step in enumerate(links.upper):
            place |= ((i >> bit) & 1) << (step + 1)
        place |= ((i >> n_up) & 1) << 2
        place |= (i >> (n_up + 1)) & 1
        place |= ((i >> (n_up + 2)) & 1) << 1
        places.append(place)
    order_p = spread(places, own_place, map_rows)
    to_own_p = order_matrix(PD, order_p)

    sigma, radius, _ = noise_terms(levels)
    chosen = jnp.where(dropped == 1, CLASSES - 1, labels)
    sig = jnp.repeat(sigma, SEQ)[:, None]
    rad = jnp.repeat(radius, SEQ)[:, None]
    clean_float = dot_f32(clean_images.reshape(rows, PD), to_own_p)
    noise_float = dot_f32(noise_draw.reshape(rows, PD), to_own_p)
    inputs = ((clean_float + sig * noise_float) / rad).astype(LOW)
    target = (sig * clean_float - SIGMA_DATA * SIGMA_DATA * noise_float) / (SIGMA_DATA * rad)
    counts = jnp.sum((groups[:, None] == groups[None, :]).astype(F32), axis=1)
    weight = 1.0 / (GROUPS * counts)

    coef = jnp.broadcast_to((2.0 * weight / (SEQ * PD))[:, None], (images, 128))


    def in_order(values, axis):
        found = []
        for i in range(line):
            index = links.index(i ^ (me // 4))
            found.append(sum(jnp.where(index == j, v, 0) for j, v in enumerate(values)))
        return jnp.concatenate(found, axis=axis)

    def cut_for_line(value):
        return [
            lax.dynamic_slice_in_dim(value, ((me // 4) ^ links.place(i)) * part, part, axis=1)
            for i in range(line)
        ]

    def seen(values):
        shape = (line, images, -1)
        return sum(
            links.seen_from_here(value.reshape(shape), i) for i, value in enumerate(values)
        ).reshape(line * images, -1)

    def run_names():
        names = jnp.stack([chosen, levels], axis=1)
        have.names = links.along([turn(names)] * line)

    def run_cond():
        names = jnp.concatenate(have.names, axis=0)
        have.chosen, have.levels = names[:, 0], names[:, 1]
        have.feats_low = noise_terms(have.levels)[2].astype(LOW)
        onehot = (have.chosen[:, None] == jnp.arange(TABLE)[None, :]).astype(LOW)
        known = jnp.concatenate([onehot, have.feats_low], axis=1)
        places = [((i & 1) << 2) | ((i >> 1) & 1) | ((i >> 2) << 1) for i in range(8)]
        order_m = order_matrix(part, spread(places, own_place % 8, map_rows))
        map_part = dot_f32(order_m, g_m.finish()).astype(LOW)
        have.map_in = map_part[:, TABLE + FOUR : TABLE + FOUR + CD]
        have.map_out = map_part[:, TABLE + FOUR + CD :]
        have.cond_zero = dot_nt(known, map_part[:, : TABLE + FOUR])
        squares = jnp.sum(have.cond_zero * have.cond_zero, axis=1, keepdims=True)
        squares = turn(jnp.broadcast_to(squares, (line * images, 128)))
        have.squares = links.along([squares] * line)

    def run_inner():
        squares = seen(turn(*have.squares))[:, :1]
        have.root = lax.rsqrt(squares * (1.0 / CD) + NORM_EPS)
        have.normed = (have.cond_zero * have.root).astype(LOW)
        have.inners = links.along(turn(*cut_for_line(dot_f32(have.normed, have.map_in))))

    def run_scales():
        have.inner = seen(turn(*have.inners))
        have.cond_low = (have.cond_zero + jax.nn.gelu(have.inner)).astype(LOW)
        scales = dot_f32(have.cond_low, have.map_out)
        scales = turn(*(scales[i * images : (i + 1) * images] for i in range(line)))
        have.scale_parts = links.along(scales)

    def run_map():
        scales = 1.0 + sum(turn(*have.scale_parts))
        have.scales = scales.reshape(images, 3, D)

    def run_patch():
        have.patch_all = assemble(g_p.finish())
        have.resid_zero = dot_f32(inputs, have.patch_all[:, :D])

    def run_in():
        rows_zero = rms_norm(have.resid_zero) * jnp.repeat(have.scales[:, 0], SEQ, axis=0)
        have.rows_zero = rows_zero.astype(LOW)
        have.project = rows_matmul(have.rows_zero, block, 3 * width, at_in)

    def run_mix():
        have.mixed = turn(attention_forward(have.project, width))

    def run_out():
        have.resid_one, have.rows_one = cols_forward(
            have.mixed, block, TILE, at_out, have.resid_zero, have.scales[:, 1]
        )

    def run_up():
        have.gated, have.hidden = expand_forward(have.rows_one, block, 2 * ff_width)

    def run_down():
        have.resid_two, have.last = cols_forward(
            have.hidden, block, TILE, at_down, have.resid_one, have.scales[:, 2]
        )

    def run_loss():
        have.squared, have.grad_low, have.grad_two, have.rows_two, have.scale_two = loss_kernel(
            have.last, have.patch_all[:, D:], target, coef, have.resid_two, have.scales[:, 2]
        )

    def start(run, parts):
        run.begin(links.reduce(*parts))

    def patch_grad(left, right):
        half, part = PD // 2, PD // 8
        own = dot_tn(left[:, :half], right).astype(LOW).reshape(2, half // 2, D)
        other = dot_tn(left[:, half:], right).astype(LOW)
        return [own] + [other[i * part : (i + 1) * part] for i in range(4)]

    def grad_down():
        start(s_s, weight_grads(from_own, this_pair, (have.rows_two, have.hidden)))

    def back_down():
        have.gated_grad = shrink_backward(have.rows_two, block, at_down, have.gated)

    def grad_up():
        start(s_e, weight_grads(from_own, this_pair, (have.rows_one, have.gated_grad)))

    def back_up():
        have.scale_one, have.grad_one, have.rows_grad = cols_backward(
            have.gated_grad, block, 2 * TILE, 0, have.resid_one, have.scales[:, 1],
            have.grad_two, (F32, LOW),
        )

    def back_out():
        have.grad_mixed = rows_matmul(have.rows_grad, block, width, at_out)

    def back_mix():
        have.grad_project = attention_backward(have.project, have.grad_mixed, width)

    def grad_in():
        start(
            s_a,
            weight_grads(
                from_own, this_pair,
                (have.rows_zero, have.grad_project), (have.rows_grad, have.mixed),
            ),
        )

    def back_in():
        have.scale_zero, have.grad_zero = cols_backward(
            have.grad_project, block, TILE, at_in, have.resid_zero, have.scales[:, 0],
            have.grad_one, (LOW,),
        )

    def grad_patch():
        parts = zip(patch_grad(inputs, have.grad_zero), patch_grad(have.grad_low, have.last))
        start(s_p, [jnp.concatenate(part, axis=-1) for part in parts])

    def back_map():
        grad_scales = jnp.stack([have.scale_zero, have.scale_one, have.scale_two], axis=1)
        scales_low = grad_scales.reshape(images, 3 * D).astype(LOW)
        have.scale_grads = links.along([turn(scales_low)] * line)

    def back_scales():
        have.scales_low = jnp.concatenate(turn(*have.scale_grads), axis=0)
        have.grad_cond = dot_nt(have.scales_low, have.map_out)
        _, pull_gelu = jax.vjp(jax.nn.gelu, have.inner)
        (grad_inner,) = pull_gelu(have.grad_cond)
        low = grad_inner.astype(LOW)
        inner = jnp.sum(low.astype(F32) * have.inner, axis=1, keepdims=True)
        have.inner_grads = links.along([low] * line)
        have.sums = links.along([jnp.broadcast_to(inner, (line * images, 128))] * line)

    def back_cond():
        grads = [
            links.seen_from_here(grad.reshape(line, images, part), i)
            for i, grad in enumerate(have.inner_grads)
        ]
        have.inner_low = in_order(grads, 2).reshape(line * images, CD)
        grad_normed = dot_nt(have.inner_low, have.map_in)
        mean = seen(have.sums)[:, :1] * (1.0 / CD)
        zero = have.root * (grad_normed - have.cond_zero * have.root * mean) + have.grad_cond
        code = jnp.stack([have.chosen // 32, have.chosen % 32], axis=1).astype(LOW)
        code = jnp.pad(code, ((0, 0), (0, 126)))
        sent = (
            have.scales_low, have.inner_low, have.feats_low, code,
            zero.astype(LOW), have.normed, have.cond_low,
        )
        rows_run.begin(links.gather_rows(jnp.concatenate(sent, axis=1)[None]))

    def grad_map():
        all_rows = rows_run.finish()
        all_rows = all_rows.reshape(-1, all_rows.shape[2])
        starts = [0]
        for size in (3 * D, CD, FOUR, 128, part, part, part):
            starts.append(starts[-1] + size)
        scales_all, inner_all, feats_all, code_all, zero_all, normed_all, cond_all = (
            all_rows[:, a:b] for a, b in zip(starts[:-1], starts[1:])
        )
        first = (own_place % 8) * map_rows
        pick = jnp.arange(part)[:, None] == first + jnp.arange(map_rows)[None, :]
        pick = pick.astype(LOW)
        zero_own = dot_f32(zero_all, pick).astype(LOW)
        normed_own = dot_f32(normed_all, pick).astype(LOW)
        cond_own = dot_f32(cond_all, pick).astype(LOW)
        code_all = code_all.astype(jnp.int32)
        chosen_all = code_all[:, 0] * 32 + code_all[:, 1]
        onehot_all = (chosen_all[:, None] == jnp.arange(CLASSES)[None, :]).astype(LOW)
        have.table_grad = dot_tn(onehot_all, zero_own)
        have.mapping_grad = jnp.concatenate(
            [
                dot_tn(zero_own, feats_all),
                dot_tn(normed_own, inner_all),
                dot_tn(cond_own, scales_all),
            ],
            axis=1,
        )

    for runs, works, held in (
        ((g_p, g_m), (run_names,), ()),
        ((g_p, g_m), (), ()),
        ((g_p, g_m), (), ()),
        ((g_p,), (run_cond,), ()),
        ((), (run_inner, run_patch), ()),
        ((), (run_scales,), ()),
        ((), (run_map,), ()),
        ((), (run_in,), ()),
        ((), (run_mix,), ()),
        ((), (run_out,), ()),
        ((), (run_up,), ()),
        ((), (run_down,), ()),
        ((), (run_loss,), ()),
        ((), (grad_down,), ()),
        ((s_s,), (back_down,), ()),
        ((s_s,), (grad_up,), ()),
        ((s_s, s_e), (back_up, back_out), ()),
        ((s_e, s_s), (back_mix, grad_in), ()),
        ((s_e, s_a), (back_in, back_map, grad_patch), (s_s,)),
        ((s_a, s_p), (back_scales,), (s_e,)),
        ((s_e, s_a, s_p), (back_cond,), ()),
        ((s_a, s_p, rows_run), (), (s_e,)),
        ((s_p, rows_run), (), (s_a,)),
        ((rows_run,), (), (s_p,)),
        ((s_a, s_p, s_e, s_s), (grad_map,), ()),
    ):
        rounds(runs, works, held)
    patch_grads = s_p.finish()
    attn_grads = s_a.finish()
    up_grad = s_e.finish().reshape(-1, ff_tiles, 2, TILE).transpose(0, 2, 1, 3)
    grads = (
        attn_grads[:, : 3 * width].reshape(inward.shape),
        attn_grads[:, 3 * width :].T,
        up_grad.reshape(expand.shape),
        s_s.finish().T,
        jnp.stack([patch_grads[:, :D], patch_grads[:, D:]]),
        have.table_grad,
        have.mapping_grad,
    )
    squares = sum((jnp.sum(grad * grad) for grad in grads))
    local_loss = jnp.sum(weight * have.squared[:, 0]) / (SEQ * PD)
    sums = links.total(jnp.stack([local_loss, squares]))
    sums = sums + rounds.token[0, :2]
    total_loss = sums[0]
    grad_norm = jnp.sqrt(sums[1])
    factor = CLIP / (grad_norm + NORM_EPS)
    count = step_count[0].astype(F32)
    fix_one = 1.0 - jnp.power(BETA_ONE, count)
    fix_two = 1.0 - jnp.power(BETA_TWO, count)
    results = [total_loss, grad_norm]
    for master, first, second, grad in zip(masters, firsts, seconds, grads):
        clipped = grad * factor
        moment = BETA_ONE * first + (1.0 - BETA_ONE) * clipped
        square = BETA_TWO * second + (1.0 - BETA_TWO) * clipped * clipped
        step_size = moment / fix_one / (jnp.sqrt(square / fix_two) + ADAM_EPS)
        results.extend([master - LEARN_RATE * (step_size + DECAY * master), moment, square])
    return tuple(results)


def solution(mesh):
    in_specs = (
        P(("dp", "tensor"), None, None),
        P(("dp", "tensor"), None, None),
        P(("dp", "tensor")),
        P(("dp", "tensor")),
        P(("dp", "tensor")),
        P(("dp", "tensor")),
        P(),
        P("dp", None, "tensor"),
        P("dp", None, "tensor"),
        P("dp", None, "tensor"),
        P("tensor", "dp"),
        P("tensor", "dp"),
        P("tensor", "dp"),
        P("dp", None, "tensor"),
        P("dp", None, "tensor"),
        P("dp", None, "tensor"),
        P("tensor", "dp"),
        P("tensor", "dp"),
        P("tensor", "dp"),
        P(None, ("dp", "tensor"), None),
        P(None, ("dp", "tensor"), None),
        P(None, ("dp", "tensor"), None),
        P(None, ("dp", "tensor")),
        P(None, ("dp", "tensor")),
        P(None, ("dp", "tensor")),
        P(("dp", "tensor"), None),
        P(("dp", "tensor"), None),
        P(("dp", "tensor"), None),
    )
    out_specs = (
        P(),
        P(),
        P("dp", None, "tensor"),
        P("dp", None, "tensor"),
        P("dp", None, "tensor"),
        P("tensor", "dp"),
        P("tensor", "dp"),
        P("tensor", "dp"),
        P("dp", None, "tensor"),
        P("dp", None, "tensor"),
        P("dp", None, "tensor"),
        P("tensor", "dp"),
        P("tensor", "dp"),
        P("tensor", "dp"),
        P(None, ("dp", "tensor"), None),
        P(None, ("dp", "tensor"), None),
        P(None, ("dp", "tensor"), None),
        P(None, ("dp", "tensor")),
        P(None, ("dp", "tensor")),
        P(None, ("dp", "tensor")),
        P(("dp", "tensor"), None),
        P(("dp", "tensor"), None),
        P(("dp", "tensor"), None),
    )
    return jax.shard_map(body, mesh=mesh, in_specs=in_specs, out_specs=out_specs, check_vma=False)
```

```python
import math
import types

import jax
import jax.numpy as jnp
from jax import lax
from jax.experimental import pallas as pl
from jax.experimental.pallas import tpu as pltpu
from jax.sharding import PartitionSpec as P

D = 1024
HEAD_DIM = 64
CD = 768
CLASSES = 1001
PD = 768
FOUR = 256
SEQ = 256
GROUPS = 4
NLEVELS = 1000
LOW = jnp.bfloat16
F32 = jnp.float32
TILE = 512
TABLE = 1024


HIGH = lax.Precision.HIGHEST
SIGMA_DATA = 0.5
LEARN_RATE = 0.05
DECAY = 0.1
BETA_ONE = 0.5
BETA_TWO = 0.5
ADAM_EPS = 1e-08
CLIP = 0.02
NORM_EPS = 1e-06
MIB = 1 << 20


def rms_norm(value):
    return value * lax.rsqrt(jnp.mean(value * value, axis=-1, keepdims=True) + NORM_EPS)


def dot_f32(left, right):
    return jnp.dot(left, right, preferred_element_type=F32)


def dot_nt(left, right):
    return lax.dot_general(left, right, (((1,), (1,)), ((), ())), preferred_element_type=F32)


def dot_tn(left, right):
    return lax.dot_general(left, right, (((0,), (0,)), ((), ())), preferred_element_type=F32)


def noise_terms(levels):
    log_sigma = -3.0 + 6.0 * levels.astype(F32) / (NLEVELS - 1)
    sigma = jnp.exp(log_sigma)
    radius = jnp.sqrt(sigma * sigma + SIGMA_DATA * SIGMA_DATA)
    half = FOUR // 2
    freqs = jnp.exp(-2.0 + 4.0 * jnp.arange(half, dtype=F32) / (half - 1))
    angles = 2.0 * math.pi * (log_sigma / 4.0)[:, None] * freqs[None, :]
    return (sigma, radius, jnp.concatenate([jnp.cos(angles), jnp.sin(angles)], axis=1))


class Rounds:
    def __init__(self, have):
        self.token = jnp.zeros((8, 128), F32)
        self.have, self.tied = have, set()

    def __call__(self, runs, works, held=()):
        fields = {name: value for name, value in vars(self.have).items() if name not in self.tied}
        values, form = jax.tree.flatten((fields, [run.waiting for run in (*runs, *held)]))
        *values, self.token = lax.optimization_barrier((*values, self.token))
        fields, waiting = jax.tree.unflatten(form, values)
        vars(self.have).update(fields)
        self.tied.update(fields)
        for run, value in zip(held, waiting[len(runs) :]):
            run.waiting = value
        for run, value in zip(runs, waiting):
            run.go_on(value)
        for work in works:
            work()


def params(vmem=50):
    return pltpu.CompilerParams(vmem_limit_bytes=vmem * MIB)


def cost(*_):
    return pl.CostEstimate(flops=1, bytes_accessed=1, transcendentals=0)


def simple(kernel, columns, in_specs, args, out_rows, out_lead=()):
    width = columns
    while width > 1024 and width % 256 == 0:
        width //= 2
    return pl.pallas_call(
        kernel,
        grid=(columns // width,),
        in_specs=[spec(width) for spec in in_specs],
        out_specs=[pl.BlockSpec((rows, width), lambda j: (0, j)) for rows in out_rows],
        out_shape=[jax.ShapeDtypeStruct((rows, columns), LOW) for rows in out_rows],
        compiler_params=params(),
        cost_estimate=cost(),
    )(*args)


def rows_spec(rows, at=0):
    return lambda width: pl.BlockSpec((rows, width), lambda j: (at, j))


def part_spec(pair, half, at):
    return lambda width: pl.BlockSpec((1, half, width), lambda j: (pair, at, j))


def even(*rows):
    return all(row % 16 == 0 for row in rows)


def one_below_other(*parts):
    rows, columns = parts[0].shape
    if not even(rows):
        return jnp.concatenate(parts, axis=0)

    def kernel(*refs):
        *refs, out_ref = refs
        for i, ref in enumerate(refs):
            out_ref[i * rows : (i + 1) * rows, :] = ref[...]

    specs = [rows_spec(rows)] * len(parts)
    return simple(kernel, columns, specs, parts, (len(parts) * rows,))[0]


def top_and_bottom(first, second):
    rows, columns = first.shape
    half = rows // 2
    if not even(half):
        return first[:half], second[half:]

    def kernel(first_ref, second_ref, top_ref, bottom_ref):
        top_ref[...] = first_ref[...]
        bottom_ref[...] = second_ref[...]

    specs = [rows_spec(half), rows_spec(half, 1)]
    return simple(kernel, columns, specs, (first, second), (half, half))


def add(*terms):
    return sum(term.astype(F32) for term in terms).astype(LOW)


def add_corners(own, came):
    _, rows, columns = own.shape
    half = rows // 2
    quarter = half // 2
    if not even(quarter):
        total = add(own[1, half:], came)
        return total[:quarter], total[quarter:]

    def kernel(own_ref, came_ref, x_ref, pair_ref):
        x_ref[...] = add(own_ref[0, :quarter], came_ref[:quarter])
        pair_ref[...] = add(own_ref[0, quarter:], came_ref[quarter:])

    specs = [part_spec(1, half, 1), rows_spec(half)]
    return simple(kernel, columns, specs, (own, came), (quarter, quarter))


def add_sides(own, came_pair, came_x, from_x, from_pair):
    _, rows, columns = own.shape
    half = rows // 2
    quarter = half // 2
    if not even(quarter):
        to_pair = add(own[1, :half], came_pair, jnp.pad(from_x, ((0, half - quarter), (0, 0))))
        to_x = add(own[0, half:], came_x, jnp.pad(from_pair, ((quarter, 0), (0, 0))))
        return to_pair, to_x

    def kernel(own_a, came_a, own_b, came_b, x_ref, pair_ref, to_pair, to_x):
        to_pair[:quarter, :] = add(own_a[0, :quarter], came_a[:quarter], x_ref[...])
        to_pair[quarter:, :] = add(own_a[0, quarter:], came_a[quarter:])
        to_x[:quarter, :] = add(own_b[0, :quarter], came_b[:quarter])
        to_x[quarter:, :] = add(own_b[0, quarter:], came_b[quarter:], pair_ref[...])

    first, second = part_spec(1, half, 0), part_spec(0, half, 1)
    side, corner = rows_spec(half), rows_spec(quarter)
    specs = [first, side, second, side, corner, corner]
    args = (own, came_pair, own, came_x, from_x, from_pair)
    return simple(kernel, columns, specs, args, (half, half))


def add_parts(count, *terms):
    columns = terms[0].shape[-1]
    rows = terms[-1].shape[0]
    size = rows // count
    cuts = [slice(i * size, (i + 1) * size) for i in range(count)]
    if not even(size):
        terms = [term[0, :rows] if term.ndim == 3 else term for term in terms]
        return tuple(add(*(term[cut] for term in terms)) for cut in cuts)

    def kernel(*refs):
        refs, outs = refs[: len(terms)], refs[len(terms) :]
        parts = [ref.at[0] if len(ref.shape) == 3 else ref for ref in refs]
        for cut, out in zip(cuts, outs):
            out[...] = add(*(part[cut, :] for part in parts))

    specs = [part_spec(0, rows, 0) if term.ndim == 3 else rows_spec(rows) for term in terms]
    return simple(kernel, columns, specs, terms, (size,) * count)


class Links:
    def __init__(self, size):
        self.size = size
        self.bits = size.bit_length() - 1
        assert 1 << self.bits == size
        self.upper = list(range(self.bits - 1, 1, -1))

    def swap(self, value, mask):
        return lax.ppermute(value, "dp", [(i, i ^ mask) for i in range(self.size)])

    def flip(self, value, bit):
        return self.swap(value, 1 << bit)

    def far(self):
        if len(self.upper) != 2:
            return None
        first, second = (1 << bit for bit in self.upper)
        return (first, second, first | second)

    def flip_pair(self, value):
        return lax.ppermute(value, "tensor", [(0, 1), (1, 0)])

    def gather(self, value, groups=((0, 1, 2),)):
        if self.far():
            (value,) = yield (value,)
            parts = [value]
            for group in groups:
                parts = [*parts] + [self.swap(value, self.far()[i]) for i in group]
                parts = yield tuple(parts)
            value = one_below_other(*parts)
        else:
            for bit in self.upper:
                (value,) = yield (value,)
                value = one_below_other(value, self.flip(value, bit))
            (value,) = yield (value,)
        by_x, by_pair = self.flip(value, 1), self.flip_pair(value)
        by_x, by_pair = yield (by_x, by_pair)
        top, bottom = top_and_bottom(by_pair, by_x)
        corner = (self.flip(top, 1), self.flip_pair(bottom))
        pieces = [value, by_x, by_pair, *corner]
        pieces = yield tuple(pieces)
        pieces = list(pieces)
        return pieces + [self.flip(piece, 0) for piece in pieces]

    def gather_rows(self, value, *groups):
        for group in groups:
            (value,) = yield (value,)
            for bit in group:
                other = self.flip_pair(value) if bit is None else self.flip(value, bit)
                value = jnp.concatenate([value, other], axis=0)
        return value


    def place(self, index):
        return sum(((index >> i) & 1) << (bit - 2) for i, bit in enumerate(self.upper))

    def index(self, place):
        return sum(((place >> (bit - 2)) & 1) << i for i, bit in enumerate(self.upper))

    def along(self, values):
        others = [
            self.swap(value, self.place(i + 1) << 2) for i, value in enumerate(values[1:])
        ]
        return [values[0], *others]

    def seen_from_here(self, value, index):
        order = [i ^ index for i in range(value.shape[0])]
        return jnp.concatenate([value[i : i + 1] for i in order], axis=0)

    def reduce(self, groups, own, *others):
        others = yield others
        corner, side, across, kept = (self.flip(others[i], 0) for i in (3, 2, 1, 0))
        (corner,) = yield (corner,)
        corner_x, corner_pair = add_corners(own, corner)
        from_x, from_pair = self.flip(corner_x, 1), self.flip_pair(corner_pair)
        from_x, from_pair, side, across = yield (from_x, from_pair, side, across)
        to_pair, to_x = add_sides(own, side, across, from_x, from_pair)
        came = kept
        terms = (own, came, self.flip_pair(to_pair), self.flip(to_x, 1))
        if self.far():
            terms = yield terms
            kept, *sent = add_parts(4, *terms)
            terms = [kept]
            for group in groups:
                terms = [*terms] + [self.swap(sent[i], self.far()[i]) for i in group]
                if group != groups[-1]:
                    terms = yield tuple(terms)
        else:
            for bit in reversed(self.upper):
                terms = yield terms
                kept, sent = add_parts(2, *terms)
                terms = (kept, self.flip(sent, bit))
        terms = yield terms
        return sum(term.astype(F32) for term in terms)

    def swap_corner(self, value):
        pairs = [(2 * i + j, 2 * (i ^ 2) + (j ^ 1)) for i in range(self.size) for j in range(2)]
        return lax.ppermute(value, ("dp", "tensor"), pairs)

    def total(self, value):
        value = value + self.flip(value, 0)
        by_x, by_pair, corner = self.flip(value, 1), self.flip_pair(value), self.swap_corner(value)
        value = (value + by_pair) + (by_x + corner)
        if self.far():
            first, second, both = (self.swap(value, mask) for mask in self.far())
            return (value + first) + (second + both)
        for bit in reversed(self.upper):
            value = value + self.flip(value, bit)
        return value


class Run:
    def __init__(self, steps=None):
        self.result = None
        if steps is not None:
            self.begin(steps)

    def begin(self, steps):
        self.steps, self.waiting = steps, next(steps)

    def go_on(self, values=None):
        values = self.waiting if values is None else values
        assert self.result is None
        try:
            self.waiting = self.steps.send(values)
        except StopIteration as stop:
            self.result = stop.value

    def finish(self):
        while self.result is None:
            self.go_on(self.waiting)
        return self.result


def reverse_bits(value, bits):
    result = 0
    for bit in range(bits):
        result |= ((value >> bit) & 1) << (bits - 1 - bit)
    return result


def spread(places, own, block):
    order = jnp.array(places, jnp.int32) ^ own
    return (order[:, None] * block + jnp.arange(block)[None, :]).reshape(-1)


def order_matrix(size, order):
    return (jnp.arange(size)[:, None] == order[None, :]).astype(LOW)


def whole(shape):
    return pl.BlockSpec(shape, lambda *_: (0,) * len(shape))


def piece_specs(pieces, width, at):
    return [pl.BlockSpec((piece.shape[0], width), lambda j: (0, at + j)) for piece in pieces]


def both_spec(rows, width, at=0):
    return pl.BlockSpec((2, rows, width), lambda j: (0, 0, at + j))


def assemble(pieces):
    starts = [0]
    for piece in pieces:
        starts.append(starts[-1] + piece.shape[0])
    columns = pieces[0].shape[1]

    def kernel(*refs):
        *refs, out_ref = refs
        for ref, start in zip(refs, starts):
            out_ref[start : start + ref.shape[0], :] = ref[...]

    return pl.pallas_call(
        kernel,
        grid=(columns // (2 * TILE),),
        in_specs=piece_specs(pieces, 2 * TILE, 0),
        out_specs=pl.BlockSpec((starts[-1], 2 * TILE), lambda j: (0, j)),
        out_shape=jax.ShapeDtypeStruct((starts[-1], columns), LOW),
        compiler_params=params(),
        cost_estimate=cost(),
    )(*pieces)


def rows_matmul(x, matrix, columns, at):
    rows = x.shape[0]

    def kernel(x_ref, matrix_ref, out_ref):
        for pair in range(2):
            out_ref[pair] = dot_f32(x_ref[...], matrix_ref[pair]).astype(LOW)

    return pl.pallas_call(
        kernel,
        grid=(columns // TILE,),
        in_specs=[whole(x.shape), both_spec(D, TILE, at)],
        out_specs=both_spec(rows, TILE),
        out_shape=jax.ShapeDtypeStruct((2, rows, columns), LOW),
        compiler_params=params(),
        cost_estimate=cost(),
    )(x, matrix)


def expand_forward(x, matrix, columns):
    rows = x.shape[0]

    def kernel(x_ref, matrix_ref, gated_ref, hidden_ref):
        for pair in range(2):
            gate = dot_f32(x_ref[...], matrix_ref[pair, :, :TILE])
            upper = dot_f32(x_ref[...], matrix_ref[pair, :, TILE:])
            gated_ref[pair, :, :TILE] = gate.astype(LOW)
            gated_ref[pair, :, TILE:] = upper.astype(LOW)
            hidden_ref[pair] = (jax.nn.gelu(gate) * upper).astype(LOW)

    return pl.pallas_call(
        kernel,
        grid=(columns // (2 * TILE),),
        in_specs=[whole(x.shape), both_spec(D, 2 * TILE)],
        out_specs=[both_spec(rows, 2 * TILE), both_spec(rows, TILE)],
        out_shape=[
            jax.ShapeDtypeStruct((2, rows, columns), LOW),
            jax.ShapeDtypeStruct((2, rows, columns // 2), LOW),
        ],
        compiler_params=params(),
        cost_estimate=cost(),
    )(x, matrix)


def gelu_parts(gate):
    root, cube = math.sqrt(2.0 / math.pi), 0.044715
    square = gate * gate
    slope = jnp.tanh(root * (gate + cube * gate * square))
    half = 0.5 * (1.0 + slope)
    turn = 0.5 * gate * (1.0 - slope * slope) * root * (1.0 + 3.0 * cube * square)
    return gate * half, half + turn


def shrink_backward(x, matrix, at, gated):
    rows = x.shape[0]
    columns = gated.shape[2] // 2

    def kernel(x_ref, gated_ref, matrix_ref, out_ref):
        for pair in range(2):
            grad = dot_f32(x_ref[...], matrix_ref[pair])
            gate = gated_ref[pair, :, :TILE].astype(F32)
            upper = gated_ref[pair, :, TILE:].astype(F32)
            value, slope = gelu_parts(gate)
            out_ref[pair, :, :TILE] = (grad * upper * slope).astype(LOW)
            out_ref[pair, :, TILE:] = (grad * value).astype(LOW)

    both = both_spec(rows, 2 * TILE)
    return pl.pallas_call(
        kernel,
        grid=(columns // TILE,),
        in_specs=[whole(x.shape), both, both_spec(D, TILE, at)],
        out_specs=both,
        out_shape=jax.ShapeDtypeStruct(gated.shape, LOW),
        compiler_params=params(),
        cost_estimate=cost(),
    )(x, gated, matrix)


def cols_sum(value_ref, matrix_ref):
    return dot_nt(value_ref[0], matrix_ref[0]) + dot_nt(value_ref[1], matrix_ref[1])


def norm_out(value, scale_ref, resid_ref, rows_ref):
    images = scale_ref.shape[0]
    resid_ref[...] = value
    for i in range(images):
        span = slice(i * SEQ, (i + 1) * SEQ)
        part = resid_ref[span, :]
        rows_ref[span, :] = (rms_norm(part) * scale_ref[i : i + 1, :]).astype(LOW)


def norm_grad(resid, scale, grad):
    root = lax.rsqrt(jnp.mean(resid * resid, axis=-1, keepdims=True) + NORM_EPS)
    normed = resid * root
    inner = grad * scale
    back = root * (inner - normed * jnp.mean(inner * normed, axis=-1, keepdims=True))
    return back, jnp.sum(grad * normed, axis=0, keepdims=True)


def cols_forward(value, matrix, width, at, resid, scale):
    _, rows, columns = value.shape
    steps = columns // width

    def kernel(value_ref, resid_ref, scale_ref, matrix_ref, out_ref, rows_ref, acc_ref):
        @pl.when(pl.program_id(0) == 0)
        def _():
            acc_ref[...] = resid_ref[...]

        acc_ref[...] += cols_sum(value_ref, matrix_ref)

        @pl.when(pl.program_id(0) == steps - 1)
        def _():
            norm_out(acc_ref[...], scale_ref, out_ref, rows_ref)

    return pl.pallas_call(
        kernel,
        grid=(steps,),
        in_specs=[
            both_spec(rows, width),
            whole(resid.shape),
            whole(scale.shape),
            both_spec(D, width, at),
        ],
        out_specs=[whole(resid.shape), whole(resid.shape)],
        out_shape=[
            jax.ShapeDtypeStruct(resid.shape, F32),
            jax.ShapeDtypeStruct(resid.shape, LOW),
        ],
        scratch_shapes=[pltpu.VMEM(resid.shape, F32)],
        compiler_params=params(),
        cost_estimate=cost(),
    )(value, resid, scale, matrix)


def cols_backward(value, matrix, width, at, resid, scale, grad, types):
    _, rows, columns = value.shape
    steps = columns // width

    def kernel(value_ref, resid_ref, scale_ref, grad_ref, matrix_ref, scale_out, *outs):
        *outs, acc_ref = outs

        @pl.when(pl.program_id(0) == 0)
        def _():
            acc_ref[...] = cols_sum(value_ref, matrix_ref)

        @pl.when(pl.program_id(0) > 0)
        def _():
            acc_ref[...] += cols_sum(value_ref, matrix_ref)

        @pl.when(pl.program_id(0) == steps - 1)
        def _():
            for i in range(scale_ref.shape[0]):
                span = slice(i * SEQ, (i + 1) * SEQ)
                back, scale_out[i : i + 1, :] = norm_grad(
                    resid_ref[span, :], scale_ref[i : i + 1, :], acc_ref[span, :]
                )
                back = back + grad_ref[span, :]
                for out in outs:
                    out[span, :] = back.astype(out.dtype)

    return pl.pallas_call(
        kernel,
        grid=(steps,),
        in_specs=[
            both_spec(rows, width),
            whole(resid.shape),
            whole(scale.shape),
            whole(resid.shape),
            both_spec(D, width, at),
        ],
        out_specs=[whole(scale.shape)] + [whole(resid.shape)] * len(types),
        out_shape=[jax.ShapeDtypeStruct(scale.shape, F32)]
        + [jax.ShapeDtypeStruct(resid.shape, kind) for kind in types],
        scratch_shapes=[pltpu.VMEM(resid.shape, F32)],
        compiler_params=params(),
        cost_estimate=cost(),
    )(value, resid, scale, grad, matrix)


def weight_grads(from_own, first, *pairs):
    rows, depth = pairs[0][0].shape
    half = depth // 2
    quarter = half // 2
    tiles = [value.shape[2] // TILE for _, value in pairs]
    starts = [sum(tiles[:i]) for i in range(len(tiles))]
    columns = sum(tiles) * TILE

    def kernel(*refs):
        count = len(pairs)
        order_ref, first_ref, *refs = refs
        x_refs, value_refs = refs[:count], refs[count : 2 * count]
        own_ref, *parts = refs[2 * count : 2 * count + 5]
        turned = refs[2 * count + 5 :]
        step = pl.program_id(0)
        for i in range(count):

            @pl.when(step == starts[i])
            def _():
                turned[i][...] = dot_nt(order_ref[...], x_refs[i][...]).astype(LOW)

            @pl.when((step >= starts[i]) & (step < starts[i] + tiles[i]))
            def _():
                for pair in range(2):
                    value = value_refs[i][first_ref[0] ^ pair]
                    own_ref[pair] = dot_f32(turned[i][:half, :], value).astype(LOW)
                    other = dot_f32(turned[i][half:, :], value).astype(LOW)
                    parts[2 * pair][...] = other[:quarter]
                    parts[2 * pair + 1][...] = other[quarter:]

    def value_spec(i):
        return pl.BlockSpec(
            (2, rows, TILE), lambda j: (0, 0, jnp.clip(j - starts[i], 0, tiles[i] - 1))
        )

    return pl.pallas_call(
        kernel,
        grid=(columns // TILE,),
        in_specs=[whole(from_own.shape), pl.BlockSpec(memory_space=pltpu.SMEM)]
        + [whole(x.shape) for x, _ in pairs]
        + [value_spec(i) for i in range(len(pairs))],
        out_specs=[pl.BlockSpec((2, half, TILE), lambda j: (0, 0, j))]
        + [pl.BlockSpec((quarter, TILE), lambda j: (0, j))] * 4,
        out_shape=[jax.ShapeDtypeStruct((2, half, columns), LOW)]
        + [jax.ShapeDtypeStruct((quarter, columns), LOW)] * 4,
        scratch_shapes=[pltpu.VMEM((depth, rows), LOW) for _ in pairs],
        compiler_params=params(),
        cost_estimate=cost(),
    )(from_own, first, *(x for x, _ in pairs), *(value for _, value in pairs))


def patch_weight_grads(*pairs):
    depth, columns = pairs[0][0].shape[1], pairs[0][1].shape[1]
    size = depth // 8

    def kernel(*refs):
        lefts, rights = refs[: len(pairs)], refs[len(pairs) : 2 * len(pairs)]
        own_ref, *parts = refs[2 * len(pairs) :]
        for i in range(len(pairs)):
            grad = dot_tn(lefts[i][...], rights[i][...]).astype(LOW)
            span = slice(i * columns, (i + 1) * columns)
            own_ref[0, :, span] = grad[: 2 * size]
            own_ref[1, :, span] = grad[2 * size : 4 * size]
            for j, part in enumerate(parts):
                part[:, span] = grad[(4 + j) * size : (5 + j) * size]

    width = len(pairs) * columns
    return pl.pallas_call(
        kernel,
        out_shape=[jax.ShapeDtypeStruct((2, 2 * size, width), LOW)]
        + [jax.ShapeDtypeStruct((size, width), LOW)] * 4,
        compiler_params=params(),
        cost_estimate=cost(),
    )(*(left for left, _ in pairs), *(right for _, right in pairs))


def head_part(ref, part):
    return ref[0, :, part * HEAD_DIM : (part + 1) * HEAD_DIM]


def softmax_turned(queries, keys):
    scores = dot_nt(keys, queries) * (1.0 / math.sqrt(HEAD_DIM))
    scores = jnp.exp(scores - jnp.max(scores, axis=0, keepdims=True))
    return scores * (1.0 / jnp.sum(scores, axis=0, keepdims=True))


def attention_specs(width):
    return [
        pl.BlockSpec((1, SEQ, width), lambda i, j, part=part: (i, j, part)) for part in range(3)
    ]


def attention_forward(project, width):
    rows = project.shape[1]

    def kernel(q_ref, k_ref, v_ref, out_ref):
        for part in range(width // HEAD_DIM):
            scores = dot_nt(head_part(q_ref, part), head_part(k_ref, part))
            scores = scores * (1.0 / math.sqrt(HEAD_DIM))
            scores = jnp.exp(scores - jnp.max(scores, axis=-1, keepdims=True))
            probs = scores * (1.0 / jnp.sum(scores, axis=-1, keepdims=True))
            mixed = dot_f32(probs.astype(LOW), head_part(v_ref, part))
            out_ref[0, :, part * HEAD_DIM : (part + 1) * HEAD_DIM] = mixed.astype(LOW)

    return pl.pallas_call(
        kernel,
        grid=(2, rows // SEQ),
        in_specs=attention_specs(width),
        out_specs=pl.BlockSpec((1, SEQ, width), lambda i, j: (i, j, 0)),
        out_shape=jax.ShapeDtypeStruct((2, rows, width), LOW),
        compiler_params=params(),
        cost_estimate=cost(8 * rows * SEQ * width, 16 * rows * width),
    )(project, project, project)


def attention_backward(project, grad, width):
    rows = project.shape[1]
    inverse_root = 1.0 / math.sqrt(HEAD_DIM)

    def kernel(q_ref, k_ref, v_ref, grad_ref, out_ref):
        for part in range(width // HEAD_DIM):
            queries, keys = head_part(q_ref, part), head_part(k_ref, part)
            values, grad = head_part(v_ref, part), head_part(grad_ref, part)
            probs = softmax_turned(queries, keys)
            grad_values = dot_f32(probs.astype(LOW), grad)
            grad_probs = dot_nt(values, grad)
            inner = jnp.sum(grad_probs * probs, axis=0, keepdims=True)
            grad_scores = (probs * (grad_probs - inner)).astype(LOW)
            grad_queries = dot_tn(keys, grad_scores).T * inverse_root
            grad_keys = dot_f32(grad_scores, queries) * inverse_root
            for place, value in enumerate((grad_queries, grad_keys, grad_values)):
                start = place * width + part * HEAD_DIM
                out_ref[0, :, start : start + HEAD_DIM] = value.astype(LOW)

    return pl.pallas_call(
        kernel,
        grid=(2, rows // SEQ),
        in_specs=attention_specs(width) + [pl.BlockSpec((1, SEQ, width), lambda i, j: (i, j, 0))],
        out_specs=pl.BlockSpec((1, SEQ, 3 * width), lambda i, j: (i, j, 0)),
        out_shape=jax.ShapeDtypeStruct((2, rows, 3 * width), LOW),
        compiler_params=params(),
        cost_estimate=cost(20 * rows * SEQ * width, 28 * rows * width),
    )(project, project, project, grad)


def loss_kernel(last, patch_out, target, coef, resid, scale):
    rows = last.shape[0]
    images = scale.shape[0]

    def kernel(
        last_ref, out_ref, target_ref, coef_ref, resid_ref, scale_ref,
        loss_ref, low_ref, grad_ref, rows_ref, scale_out,
    ):
        for i in range(images):
            span = slice(i * SEQ, (i + 1) * SEQ)
            diff = dot_nt(last_ref[span, :], out_ref[...]) - target_ref[span, :]
            total = jnp.sum(jnp.sum(diff * diff, axis=1, keepdims=True), axis=0, keepdims=True)
            loss_ref[i : i + 1, :] = jnp.broadcast_to(total, (1, 128))
            low = (diff * coef_ref[i : i + 1, :1]).astype(LOW)
            low_ref[span, :] = low
            back, scale_out[i : i + 1, :] = norm_grad(
                resid_ref[span, :], scale_ref[i : i + 1, :], dot_f32(low, out_ref[...])
            )
            grad_ref[span, :] = back
            rows_ref[span, :] = back.astype(LOW)

    return pl.pallas_call(
        kernel,
        out_shape=[
            jax.ShapeDtypeStruct((images, 128), F32),
            jax.ShapeDtypeStruct((rows, PD), LOW),
            jax.ShapeDtypeStruct((rows, D), F32),
            jax.ShapeDtypeStruct((rows, D), LOW),
            jax.ShapeDtypeStruct((images, D), F32),
        ],
        compiler_params=params(),
        cost_estimate=cost(4 * rows * D * PD, 16 * rows * D),
    )(last, patch_out, target, coef, resid, scale)


def body(
    clean_images,
    noise_draw,
    levels,
    labels,
    dropped,
    groups,
    step_count,
    inward,
    first_inward,
    second_inward,
    outward,
    first_outward,
    second_outward,
    expand,
    first_expand,
    second_expand,
    shrink,
    first_shrink,
    second_shrink,
    patches,
    first_patches,
    second_patches,
    classes,
    first_classes,
    second_classes,
    mapping,
    first_mapping,
    second_mapping,
):
    masters = (inward, outward, expand, shrink, patches, classes, mapping)
    firsts = (
        first_inward,
        first_outward,
        first_expand,
        first_shrink,
        first_patches,
        first_classes,
        first_mapping,
    )
    seconds = (
        second_inward,
        second_outward,
        second_expand,
        second_shrink,
        second_patches,
        second_classes,
        second_mapping,
    )
    links = Links(lax.axis_size("dp"))
    me, pair = lax.axis_index("dp"), lax.axis_index("tensor")
    own_place = me * 2 + pair
    images = clean_images.shape[0]
    rows = images * SEQ
    width = inward.shape[2]
    ff_width = expand.shape[2]
    ff_tiles = ff_width // TILE
    map_rows = mapping.shape[0]

    have = types.SimpleNamespace()
    rounds = Rounds(have)

    def turn(*values):
        return values[0] if len(values) == 1 else values

    flat_patch = jnp.concatenate([patches[0], patches[1]], axis=1).astype(LOW)
    table = jnp.pad(classes.T, ((0, 0), (0, TABLE - CLASSES)))
    flat_map = jnp.concatenate([table, mapping], axis=1).astype(LOW)
    flat_up = expand.reshape(-1, 2, ff_tiles, TILE).transpose(0, 2, 1, 3)
    flat = jnp.concatenate(
        [
            flat_up.reshape(expand.shape[0], -1),
            shrink.T,
            inward.reshape(inward.shape[0], -1),
            outward.T,
        ],
        axis=1,
    ).astype(LOW)
    block = lax.all_gather(flat, ("tensor", "dp"), axis=0, tiled=True)
    block = block.reshape(2, D, flat.shape[1])
    at_down = 2 * ff_tiles
    at_in = 3 * ff_tiles
    at_out = at_in + 3 * width // TILE
    g_p = Run(links.gather(flat_patch))
    g_m = Run(links.gather_rows(flat_map, (1,), (None,), (0,)))
    s_p, s_a, s_e, s_s, rows_run = (Run() for _ in range(5))
    line = links.size // 4
    part = 8 * map_rows

    n_up = len(links.upper)

    order_d = spread([reverse_bits(i, links.bits) for i in range(links.size)], me, D // links.size)
    to_own = order_matrix(D, order_d)
    from_own = to_own.T
    this_pair = pair.reshape(1)
    places = []
    for i in range(2 * links.size):
        place = 0
        for bit, step in enumerate(links.upper):
            place |= ((i >> bit) & 1) << (step + 1)
        place |= ((i >> n_up) & 1) << 2
        place |= (i >> (n_up + 1)) & 1
        place |= ((i >> (n_up + 2)) & 1) << 1
        places.append(place)
    order_p = spread(places, own_place, map_rows)
    to_own_p = order_matrix(PD, order_p)

    sigma, radius, _ = noise_terms(levels)
    chosen = jnp.where(dropped == 1, CLASSES - 1, labels)
    sig = jnp.repeat(sigma, SEQ)[:, None]
    rad = jnp.repeat(radius, SEQ)[:, None]
    clean_float = dot_f32(clean_images.reshape(rows, PD), to_own_p)
    noise_float = dot_f32(noise_draw.reshape(rows, PD), to_own_p)
    inputs = ((clean_float + sig * noise_float) / rad).astype(LOW)
    target = (sig * clean_float - SIGMA_DATA * SIGMA_DATA * noise_float) / (SIGMA_DATA * rad)
    counts = jnp.sum((groups[:, None] == groups[None, :]).astype(F32), axis=1)
    weight = 1.0 / (GROUPS * counts)

    coef = jnp.broadcast_to((2.0 * weight / (SEQ * PD))[:, None], (images, 128))


    def in_order(values, axis):
        found = []
        for i in range(line):
            index = links.index(i ^ (me // 4))
            found.append(sum(jnp.where(index == j, v, 0) for j, v in enumerate(values)))
        return jnp.concatenate(found, axis=axis)

    def cut_for_line(value):
        return [
            lax.dynamic_slice_in_dim(value, ((me // 4) ^ links.place(i)) * part, part, axis=1)
            for i in range(line)
        ]

    def seen(values):
        shape = (line, images, -1)
        return sum(
            links.seen_from_here(value.reshape(shape), i) for i, value in enumerate(values)
        ).reshape(line * images, -1)

    def run_names():
        names = jnp.stack([chosen, levels], axis=1)
        have.names = links.along([turn(names)] * line)

    def run_cond():
        names = jnp.concatenate(have.names, axis=0)
        have.chosen, have.levels = names[:, 0], names[:, 1]
        have.feats_low = noise_terms(have.levels)[2].astype(LOW)
        onehot = (have.chosen[:, None] == jnp.arange(TABLE)[None, :]).astype(LOW)
        known = jnp.concatenate([onehot, have.feats_low], axis=1)
        places = [((i & 1) << 2) | ((i >> 1) & 1) | ((i >> 2) << 1) for i in range(8)]
        order_m = order_matrix(part, spread(places, own_place % 8, map_rows))
        map_part = dot_f32(order_m, g_m.finish()).astype(LOW)
        have.map_in = map_part[:, TABLE + FOUR : TABLE + FOUR + CD]
        have.map_out = map_part[:, TABLE + FOUR + CD :]
        have.cond_zero = dot_nt(known, map_part[:, : TABLE + FOUR])
        squares = jnp.sum(have.cond_zero * have.cond_zero, axis=1, keepdims=True)
        squares = turn(jnp.broadcast_to(squares, (line * images, 128)))
        have.squares = links.along([squares] * line)

    def run_inner():
        squares = seen(turn(*have.squares))[:, :1]
        have.root = lax.rsqrt(squares * (1.0 / CD) + NORM_EPS)
        have.normed = (have.cond_zero * have.root).astype(LOW)
        have.inners = links.along(turn(*cut_for_line(dot_f32(have.normed, have.map_in))))

    def run_scales():
        have.inner = seen(turn(*have.inners))
        have.cond_low = (have.cond_zero + jax.nn.gelu(have.inner)).astype(LOW)
        scales = dot_f32(have.cond_low, have.map_out)
        scales = turn(*(scales[i * images : (i + 1) * images] for i in range(line)))
        have.scale_parts = links.along(scales)

    def run_map():
        scales = 1.0 + sum(turn(*have.scale_parts))
        have.scales = scales.reshape(images, 3, D)

    def run_patch():
        have.patch_all = assemble(g_p.finish())
        have.resid_zero = dot_f32(inputs, have.patch_all[:, :D])

    def run_in():
        rows_zero = rms_norm(have.resid_zero) * jnp.repeat(have.scales[:, 0], SEQ, axis=0)
        have.rows_zero = rows_zero.astype(LOW)
        have.project = rows_matmul(have.rows_zero, block, 3 * width, at_in)

    def run_mix():
        have.mixed = turn(attention_forward(have.project, width))

    def run_out():
        have.resid_one, have.rows_one = cols_forward(
            have.mixed, block, TILE, at_out, have.resid_zero, have.scales[:, 1]
        )

    def run_up():
        have.gated, have.hidden = expand_forward(have.rows_one, block, 2 * ff_width)

    def run_down():
        have.resid_two, have.last = cols_forward(
            have.hidden, block, TILE, at_down, have.resid_one, have.scales[:, 2]
        )

    def run_loss():
        have.squared, have.grad_low, have.grad_two, have.rows_two, have.scale_two = loss_kernel(
            have.last, have.patch_all[:, D:], target, coef, have.resid_two, have.scales[:, 2]
        )

    def start(run, parts, groups=((0, 1, 2),)):
        run.begin(links.reduce(groups, *parts))

    def grad_down():
        start(s_s, weight_grads(from_own, this_pair, (have.rows_two, have.hidden)))

    def back_down():
        have.gated_grad = shrink_backward(have.rows_two, block, at_down, have.gated)

    def grad_up():
        parts = weight_grads(from_own, this_pair, (have.rows_one, have.gated_grad))
        start(s_e, parts, ((0,), (1, 2)))

    def back_up():
        have.scale_one, have.grad_one, have.rows_grad = cols_backward(
            have.gated_grad, block, 2 * TILE, 0, have.resid_one, have.scales[:, 1],
            have.grad_two, (F32, LOW),
        )

    def back_out():
        have.grad_mixed = rows_matmul(have.rows_grad, block, width, at_out)

    def back_mix():
        have.grad_project = attention_backward(have.project, have.grad_mixed, width)

    def grad_in():
        start(
            s_a,
            weight_grads(
                from_own, this_pair,
                (have.rows_zero, have.grad_project), (have.rows_grad, have.mixed),
            ),
        )

    def back_in():
        have.scale_zero, have.grad_zero = cols_backward(
            have.grad_project, block, TILE, at_in, have.resid_zero, have.scales[:, 0],
            have.grad_one, (LOW,),
        )

    def grad_patch():
        pairs = ((inputs, have.grad_zero), (have.grad_low, have.last))
        start(s_p, patch_weight_grads(*pairs))

    def back_map():
        grad_scales = jnp.stack([have.scale_zero, have.scale_one, have.scale_two], axis=1)
        scales_low = grad_scales.reshape(images, 3 * D).astype(LOW)
        have.scale_grads = links.along([turn(scales_low)] * line)

    def back_scales():
        have.scales_low = jnp.concatenate(turn(*have.scale_grads), axis=0)
        have.grad_cond = dot_nt(have.scales_low, have.map_out)
        _, pull_gelu = jax.vjp(jax.nn.gelu, have.inner)
        (grad_inner,) = pull_gelu(have.grad_cond)
        low = grad_inner.astype(LOW)
        inner = jnp.sum(low.astype(F32) * have.inner, axis=1, keepdims=True)
        have.inner_grads = links.along([low] * line)
        have.sums = links.along([jnp.broadcast_to(inner, (line * images, 128))] * line)

    def back_cond():
        grads = [
            links.seen_from_here(grad.reshape(line, images, part), i)
            for i, grad in enumerate(have.inner_grads)
        ]
        have.inner_low = in_order(grads, 2).reshape(line * images, CD)
        grad_normed = dot_nt(have.inner_low, have.map_in)
        mean = seen(have.sums)[:, :1] * (1.0 / CD)
        zero = have.root * (grad_normed - have.cond_zero * have.root * mean) + have.grad_cond
        code = jnp.stack([have.chosen // 32, have.chosen % 32], axis=1).astype(LOW)
        code = jnp.pad(code, ((0, 0), (0, 126)))
        sent = (
            have.scales_low, have.inner_low, have.feats_low, code,
            zero.astype(LOW), have.normed, have.cond_low,
        )
        rows_run.begin(links.gather_rows(jnp.concatenate(sent, axis=1)[None], (0, 1), (None,)))

    def grad_map():
        all_rows = rows_run.finish()
        all_rows = all_rows.reshape(-1, all_rows.shape[2])
        starts = [0]
        for size in (3 * D, CD, FOUR, 128, part, part, part):
            starts.append(starts[-1] + size)
        scales_all, inner_all, feats_all, code_all, zero_all, normed_all, cond_all = (
            all_rows[:, a:b] for a, b in zip(starts[:-1], starts[1:])
        )
        first = (own_place % 8) * map_rows
        pick = jnp.arange(part)[:, None] == first + jnp.arange(map_rows)[None, :]
        pick = pick.astype(LOW)
        zero_own = dot_f32(zero_all, pick).astype(LOW)
        normed_own = dot_f32(normed_all, pick).astype(LOW)
        cond_own = dot_f32(cond_all, pick).astype(LOW)
        code_all = code_all.astype(jnp.int32)
        chosen_all = code_all[:, 0] * 32 + code_all[:, 1]
        onehot_all = (chosen_all[:, None] == jnp.arange(CLASSES)[None, :]).astype(LOW)
        have.table_grad = dot_tn(onehot_all, zero_own)
        have.mapping_grad = jnp.concatenate(
            [
                dot_tn(zero_own, feats_all),
                dot_tn(normed_own, inner_all),
                dot_tn(cond_own, scales_all),
            ],
            axis=1,
        )

    def more_p():
        s_p.go_on()

    def more_r():
        rows_run.go_on()

    for runs, works, held in (
        ((g_p, g_m), (run_names,), ()),
        ((g_p, g_m), (), ()),
        ((g_p, g_m), (), ()),
        ((g_p,), (run_cond,), ()),
        ((), (run_inner, run_patch), ()),
        ((), (run_scales,), ()),
        ((), (run_map,), ()),
        ((), (run_in,), ()),
        ((), (run_mix,), ()),
        ((), (run_out,), ()),
        ((), (run_up,), ()),
        ((), (run_down,), ()),
        ((), (run_loss,), ()),
        ((), (grad_down,), ()),
        ((s_s,), (back_down,), ()),
        ((s_s,), (grad_up,), ()),
        ((s_s, s_e), (back_up, back_out), ()),
        ((s_e,), (back_mix, grad_in), ()),
        ((s_e, s_a, s_s), (back_in, back_map, grad_patch), ()),
        ((s_a, s_p, s_e), (back_scales, more_p), (s_s,)),
        ((s_a, s_e, s_p), (), ()),
        ((s_a, s_p), (back_cond, more_r), (s_e,)),
        ((rows_run,), (), ()),
        ((s_a, s_p, s_e, s_s), (grad_map,), ()),
    ):
        rounds(runs, works, held)
    patch_grads = s_p.finish()
    attn_grads = s_a.finish()
    up_grad = s_e.finish().reshape(-1, ff_tiles, 2, TILE).transpose(0, 2, 1, 3)
    grads = (
        attn_grads[:, : 3 * width].reshape(inward.shape),
        attn_grads[:, 3 * width :].T,
        up_grad.reshape(expand.shape),
        s_s.finish().T,
        jnp.stack([patch_grads[:, :D], patch_grads[:, D:]]),
        have.table_grad,
        have.mapping_grad,
    )
    squares = sum((jnp.sum(grad * grad) for grad in grads))
    local_loss = jnp.sum(weight * have.squared[:, 0]) / (SEQ * PD)
    sums = links.total(jnp.stack([local_loss, squares]))
    sums = sums + rounds.token[0, :2]
    total_loss = sums[0]
    grad_norm = jnp.sqrt(sums[1])
    factor = CLIP / (grad_norm + NORM_EPS)
    count = step_count[0].astype(F32)
    fix_one = 1.0 - jnp.power(BETA_ONE, count)
    fix_two = 1.0 - jnp.power(BETA_TWO, count)
    results = [total_loss, grad_norm]
    for master, first, second, grad in zip(masters, firsts, seconds, grads):
        clipped = grad * factor
        moment = BETA_ONE * first + (1.0 - BETA_ONE) * clipped
        square = BETA_TWO * second + (1.0 - BETA_TWO) * clipped * clipped
        step_size = moment / fix_one / (jnp.sqrt(square / fix_two) + ADAM_EPS)
        results.extend([master - LEARN_RATE * (step_size + DECAY * master), moment, square])
    return tuple(results)


def solution(mesh):
    in_specs = (
        P(("dp", "tensor"), None, None),
        P(("dp", "tensor"), None, None),
        P(("dp", "tensor")),
        P(("dp", "tensor")),
        P(("dp", "tensor")),
        P(("dp", "tensor")),
        P(),
        P("dp", None, "tensor"),
        P("dp", None, "tensor"),
        P("dp", None, "tensor"),
        P("tensor", "dp"),
        P("tensor", "dp"),
        P("tensor", "dp"),
        P("dp", None, "tensor"),
        P("dp", None, "tensor"),
        P("dp", None, "tensor"),
        P("tensor", "dp"),
        P("tensor", "dp"),
        P("tensor", "dp"),
        P(None, ("dp", "tensor"), None),
        P(None, ("dp", "tensor"), None),
        P(None, ("dp", "tensor"), None),
        P(None, ("dp", "tensor")),
        P(None, ("dp", "tensor")),
        P(None, ("dp", "tensor")),
        P(("dp", "tensor"), None),
        P(("dp", "tensor"), None),
        P(("dp", "tensor"), None),
    )
    out_specs = (
        P(),
        P(),
        P("dp", None, "tensor"),
        P("dp", None, "tensor"),
        P("dp", None, "tensor"),
        P("tensor", "dp"),
        P("tensor", "dp"),
        P("tensor", "dp"),
        P("dp", None, "tensor"),
        P("dp", None, "tensor"),
        P("dp", None, "tensor"),
        P("tensor", "dp"),
        P("tensor", "dp"),
        P("tensor", "dp"),
        P(None, ("dp", "tensor"), None),
        P(None, ("dp", "tensor"), None),
        P(None, ("dp", "tensor"), None),
        P(None, ("dp", "tensor")),
        P(None, ("dp", "tensor")),
        P(None, ("dp", "tensor")),
        P(("dp", "tensor"), None),
        P(("dp", "tensor"), None),
        P(("dp", "tensor"), None),
    )
    return jax.shard_map(body, mesh=mesh, in_specs=in_specs, out_specs=out_specs, check_vma=False)
```

```python
import math
import types

import jax
import jax.numpy as jnp
from jax import lax
from jax.experimental import pallas as pl
from jax.experimental.pallas import tpu as pltpu
from jax.sharding import PartitionSpec as P

D = 1024
HEAD_DIM = 64
CD = 768
CLASSES = 1001
PD = 768
FOUR = 256
SEQ = 256
GROUPS = 4
NLEVELS = 1000
LOW = jnp.bfloat16
F32 = jnp.float32
TILE = 512
TABLE = 1024


HIGH = lax.Precision.HIGHEST
SIGMA_DATA = 0.5
LEARN_RATE = 0.05
DECAY = 0.1
BETA_ONE = 0.5
BETA_TWO = 0.5
ADAM_EPS = 1e-08
CLIP = 0.02
NORM_EPS = 1e-06
MIB = 1 << 20


def rms_norm(value):
    return value * lax.rsqrt(jnp.mean(value * value, axis=-1, keepdims=True) + NORM_EPS)


def dot_f32(left, right):
    return jnp.dot(left, right, preferred_element_type=F32)


def dot_nt(left, right):
    return lax.dot_general(left, right, (((1,), (1,)), ((), ())), preferred_element_type=F32)


def dot_tn(left, right):
    return lax.dot_general(left, right, (((0,), (0,)), ((), ())), preferred_element_type=F32)


def noise_terms(levels):
    log_sigma = -3.0 + 6.0 * levels.astype(F32) / (NLEVELS - 1)
    sigma = jnp.exp(log_sigma)
    radius = jnp.sqrt(sigma * sigma + SIGMA_DATA * SIGMA_DATA)
    half = FOUR // 2
    freqs = jnp.exp(-2.0 + 4.0 * jnp.arange(half, dtype=F32) / (half - 1))
    angles = 2.0 * math.pi * (log_sigma / 4.0)[:, None] * freqs[None, :]
    return (sigma, radius, jnp.concatenate([jnp.cos(angles), jnp.sin(angles)], axis=1))


class Rounds:
    def __init__(self, have):
        self.token = jnp.zeros((8, 128), F32)
        self.have, self.tied = have, set()

    def __call__(self, runs, works, held=()):
        fields = {name: value for name, value in vars(self.have).items() if name not in self.tied}
        values, form = jax.tree.flatten((fields, [run.waiting for run in (*runs, *held)]))
        *values, self.token = lax.optimization_barrier((*values, self.token))
        fields, waiting = jax.tree.unflatten(form, values)
        vars(self.have).update(fields)
        self.tied.update(fields)
        for run, value in zip(held, waiting[len(runs) :]):
            run.waiting = value
        for run, value in zip(runs, waiting):
            run.go_on(value)
        for work in works:
            work()


def params(vmem=48):
    return pltpu.CompilerParams(vmem_limit_bytes=vmem * MIB)


def cost(*_):
    return pl.CostEstimate(flops=1, bytes_accessed=1, transcendentals=0)


def simple(kernel, columns, in_specs, args, out_rows, out_lead=()):
    width = columns
    while width > 1024 and width % 256 == 0:
        width //= 2
    return pl.pallas_call(
        kernel,
        grid=(columns // width,),
        in_specs=[spec(width) for spec in in_specs],
        out_specs=[pl.BlockSpec((rows, width), lambda j: (0, j)) for rows in out_rows],
        out_shape=[jax.ShapeDtypeStruct((rows, columns), LOW) for rows in out_rows],
        compiler_params=params(),
        cost_estimate=cost(),
    )(*args)


def rows_spec(rows, at=0):
    return lambda width: pl.BlockSpec((rows, width), lambda j: (at, j))


def part_spec(pair, half, at):
    return lambda width: pl.BlockSpec((1, half, width), lambda j: (pair, at, j))


def even(*rows):
    return all(row % 16 == 0 for row in rows)


def one_below_other(*parts):
    rows, columns = parts[0].shape
    if not even(rows):
        return jnp.concatenate(parts, axis=0)

    def kernel(*refs):
        *refs, out_ref = refs
        for i, ref in enumerate(refs):
            out_ref[i * rows : (i + 1) * rows, :] = ref[...]

    specs = [rows_spec(rows)] * len(parts)
    return simple(kernel, columns, specs, parts, (len(parts) * rows,))[0]


def top_and_bottom(first, second):
    rows, columns = first.shape
    half = rows // 2
    if not even(half):
        return first[:half], second[half:]

    def kernel(first_ref, second_ref, top_ref, bottom_ref):
        top_ref[...] = first_ref[...]
        bottom_ref[...] = second_ref[...]

    specs = [rows_spec(half), rows_spec(half, 1)]
    return simple(kernel, columns, specs, (first, second), (half, half))


def add(*terms):
    return sum(term.astype(F32) for term in terms).astype(LOW)


def add_corners(own, came):
    _, rows, columns = own.shape
    half = rows // 2
    quarter = half // 2
    if not even(quarter):
        total = add(own[1, half:], came)
        return total[:quarter], total[quarter:]

    def kernel(own_ref, came_ref, x_ref, pair_ref):
        x_ref[...] = add(own_ref[0, :quarter], came_ref[:quarter])
        pair_ref[...] = add(own_ref[0, quarter:], came_ref[quarter:])

    specs = [part_spec(1, half, 1), rows_spec(half)]
    return simple(kernel, columns, specs, (own, came), (quarter, quarter))


def add_sides(own, came_pair, came_x, from_x, from_pair):
    _, rows, columns = own.shape
    half = rows // 2
    quarter = half // 2
    if not even(quarter):
        to_pair = add(own[1, :half], came_pair, jnp.pad(from_x, ((0, half - quarter), (0, 0))))
        to_x = add(own[0, half:], came_x, jnp.pad(from_pair, ((quarter, 0), (0, 0))))
        return to_pair, to_x

    def kernel(own_a, came_a, own_b, came_b, x_ref, pair_ref, to_pair, to_x):
        to_pair[:quarter, :] = add(own_a[0, :quarter], came_a[:quarter], x_ref[...])
        to_pair[quarter:, :] = add(own_a[0, quarter:], came_a[quarter:])
        to_x[:quarter, :] = add(own_b[0, :quarter], came_b[:quarter])
        to_x[quarter:, :] = add(own_b[0, quarter:], came_b[quarter:], pair_ref[...])

    first, second = part_spec(1, half, 0), part_spec(0, half, 1)
    side, corner = rows_spec(half), rows_spec(quarter)
    specs = [first, side, second, side, corner, corner]
    args = (own, came_pair, own, came_x, from_x, from_pair)
    return simple(kernel, columns, specs, args, (half, half))


def add_parts(count, *terms):
    columns = terms[0].shape[-1]
    rows = terms[-1].shape[0]
    size = rows // count
    cuts = [slice(i * size, (i + 1) * size) for i in range(count)]
    if not even(size):
        terms = [term[0, :rows] if term.ndim == 3 else term for term in terms]
        return tuple(add(*(term[cut] for term in terms)) for cut in cuts)

    def kernel(*refs):
        refs, outs = refs[: len(terms)], refs[len(terms) :]
        parts = [ref.at[0] if len(ref.shape) == 3 else ref for ref in refs]
        for cut, out in zip(cuts, outs):
            out[...] = add(*(part[cut, :] for part in parts))

    specs = [part_spec(0, rows, 0) if term.ndim == 3 else rows_spec(rows) for term in terms]
    return simple(kernel, columns, specs, terms, (size,) * count)


class Links:
    def __init__(self, size):
        self.size = size
        self.bits = size.bit_length() - 1
        assert 1 << self.bits == size
        self.upper = list(range(self.bits - 1, 1, -1))

    def swap(self, value, mask):
        return lax.ppermute(value, "dp", [(i, i ^ mask) for i in range(self.size)])

    def flip(self, value, bit):
        return self.swap(value, 1 << bit)

    def far(self):
        if len(self.upper) != 2:
            return None
        first, second = (1 << bit for bit in self.upper)
        return (first, second, first | second)

    def flip_pair(self, value):
        return lax.ppermute(value, "tensor", [(0, 1), (1, 0)])

    def gather(self, value, groups=((0, 1, 2),)):
        if self.far():
            (value,) = yield (value,)
            parts = [value]
            for group in groups:
                parts = [*parts] + [self.swap(value, self.far()[i]) for i in group]
                parts = yield tuple(parts)
            value = one_below_other(*parts)
        else:
            for bit in self.upper:
                (value,) = yield (value,)
                value = one_below_other(value, self.flip(value, bit))
            (value,) = yield (value,)
        by_x, by_pair = self.flip(value, 1), self.flip_pair(value)
        by_x, by_pair = yield (by_x, by_pair)
        top, bottom = top_and_bottom(by_pair, by_x)
        corner = (self.flip(top, 1), self.flip_pair(bottom))
        pieces = [value, by_x, by_pair, *corner]
        pieces = yield tuple(pieces)
        pieces = list(pieces)
        return pieces + [self.flip(piece, 0) for piece in pieces]

    def gather_rows(self, value, *groups):
        for group in groups:
            (value,) = yield (value,)
            for bit in group:
                other = self.flip_pair(value) if bit is None else self.flip(value, bit)
                value = jnp.concatenate([value, other], axis=0)
        return value


    def place(self, index):
        return sum(((index >> i) & 1) << (bit - 2) for i, bit in enumerate(self.upper))

    def index(self, place):
        return sum(((place >> (bit - 2)) & 1) << i for i, bit in enumerate(self.upper))

    def along(self, values):
        others = [
            self.swap(value, self.place(i + 1) << 2) for i, value in enumerate(values[1:])
        ]
        return [values[0], *others]

    def seen_from_here(self, value, index):
        order = [i ^ index for i in range(value.shape[0])]
        return jnp.concatenate([value[i : i + 1] for i in order], axis=0)

    def reduce(self, groups, own, *others):
        others = yield others
        corner, side, across, kept = (self.flip(others[i], 0) for i in (3, 2, 1, 0))
        (corner,) = yield (corner,)
        corner_x, corner_pair = add_corners(own, corner)
        from_x, from_pair = self.flip(corner_x, 1), self.flip_pair(corner_pair)
        from_x, from_pair, side, across = yield (from_x, from_pair, side, across)
        to_pair, to_x = add_sides(own, side, across, from_x, from_pair)
        came = kept
        terms = (own, came, self.flip_pair(to_pair), self.flip(to_x, 1))
        if self.far():
            terms = yield terms
            kept, *sent = add_parts(4, *terms)
            terms = [kept]
            for group in groups:
                terms = [*terms] + [self.swap(sent[i], self.far()[i]) for i in group]
                if group != groups[-1]:
                    terms = yield tuple(terms)
        else:
            for bit in reversed(self.upper):
                terms = yield terms
                kept, sent = add_parts(2, *terms)
                terms = (kept, self.flip(sent, bit))
        terms = yield terms
        return sum(term.astype(F32) for term in terms)

    def swap_corner(self, value):
        pairs = [(2 * i + j, 2 * (i ^ 2) + (j ^ 1)) for i in range(self.size) for j in range(2)]
        return lax.ppermute(value, ("dp", "tensor"), pairs)

    def total(self, value):
        value = value + self.flip(value, 0)
        by_x, by_pair, corner = self.flip(value, 1), self.flip_pair(value), self.swap_corner(value)
        value = (value + by_pair) + (by_x + corner)
        if self.far():
            first, second, both = (self.swap(value, mask) for mask in self.far())
            return (value + first) + (second + both)
        for bit in reversed(self.upper):
            value = value + self.flip(value, bit)
        return value


class Run:
    def __init__(self, steps=None):
        self.result = None
        if steps is not None:
            self.begin(steps)

    def begin(self, steps):
        self.steps, self.waiting = steps, next(steps)

    def go_on(self, values=None):
        values = self.waiting if values is None else values
        assert self.result is None
        try:
            self.waiting = self.steps.send(values)
        except StopIteration as stop:
            self.result = stop.value

    def finish(self):
        while self.result is None:
            self.go_on(self.waiting)
        return self.result


def reverse_bits(value, bits):
    result = 0
    for bit in range(bits):
        result |= ((value >> bit) & 1) << (bits - 1 - bit)
    return result


def spread(places, own, block):
    order = jnp.array(places, jnp.int32) ^ own
    return (order[:, None] * block + jnp.arange(block)[None, :]).reshape(-1)


def order_matrix(size, order):
    return (jnp.arange(size)[:, None] == order[None, :]).astype(LOW)


def whole(shape):
    return pl.BlockSpec(shape, lambda *_: (0,) * len(shape))


def piece_specs(pieces, width, at):
    return [pl.BlockSpec((piece.shape[0], width), lambda j: (0, at + j)) for piece in pieces]


def both_spec(rows, width, at=0):
    return pl.BlockSpec((2, rows, width), lambda j: (0, 0, at + j))


def assemble(pieces):
    starts = [0]
    for piece in pieces:
        starts.append(starts[-1] + piece.shape[0])
    columns = pieces[0].shape[1]

    def kernel(*refs):
        *refs, out_ref = refs
        for ref, start in zip(refs, starts):
            out_ref[start : start + ref.shape[0], :] = ref[...]

    return pl.pallas_call(
        kernel,
        grid=(columns // (2 * TILE),),
        in_specs=piece_specs(pieces, 2 * TILE, 0),
        out_specs=pl.BlockSpec((starts[-1], 2 * TILE), lambda j: (0, j)),
        out_shape=jax.ShapeDtypeStruct((starts[-1], columns), LOW),
        compiler_params=params(),
        cost_estimate=cost(),
    )(*pieces)


def rows_matmul(x, matrix, columns, at):
    rows = x.shape[0]

    def kernel(x_ref, matrix_ref, out_ref):
        for pair in range(2):
            out_ref[pair] = dot_f32(x_ref[...], matrix_ref[pair]).astype(LOW)

    return pl.pallas_call(
        kernel,
        grid=(columns // TILE,),
        in_specs=[whole(x.shape), both_spec(D, TILE, at)],
        out_specs=both_spec(rows, TILE),
        out_shape=jax.ShapeDtypeStruct((2, rows, columns), LOW),
        compiler_params=params(),
        cost_estimate=cost(),
    )(x, matrix)


def expand_forward(x, matrix, columns):
    rows = x.shape[0]

    def kernel(x_ref, matrix_ref, gated_ref, hidden_ref):
        for pair in range(2):
            gate = dot_f32(x_ref[...], matrix_ref[pair, :, :TILE])
            upper = dot_f32(x_ref[...], matrix_ref[pair, :, TILE:])
            gated_ref[pair, :, :TILE] = gate.astype(LOW)
            gated_ref[pair, :, TILE:] = upper.astype(LOW)
            hidden_ref[pair] = (jax.nn.gelu(gate) * upper).astype(LOW)

    return pl.pallas_call(
        kernel,
        grid=(columns // (2 * TILE),),
        in_specs=[whole(x.shape), both_spec(D, 2 * TILE)],
        out_specs=[both_spec(rows, 2 * TILE), both_spec(rows, TILE)],
        out_shape=[
            jax.ShapeDtypeStruct((2, rows, columns), LOW),
            jax.ShapeDtypeStruct((2, rows, columns // 2), LOW),
        ],
        compiler_params=params(),
        cost_estimate=cost(),
    )(x, matrix)


def gelu_parts(gate):
    root, cube = math.sqrt(2.0 / math.pi), 0.044715
    square = gate * gate
    slope = jnp.tanh(root * (gate + cube * gate * square))
    half = 0.5 * (1.0 + slope)
    turn = 0.5 * gate * (1.0 - slope * slope) * root * (1.0 + 3.0 * cube * square)
    return gate * half, half + turn


def shrink_backward(x, matrix, at, gated):
    rows = x.shape[0]
    columns = gated.shape[2] // 2

    def kernel(x_ref, gated_ref, matrix_ref, out_ref):
        for pair in range(2):
            grad = dot_f32(x_ref[...], matrix_ref[pair])
            gate = gated_ref[pair, :, :TILE].astype(F32)
            upper = gated_ref[pair, :, TILE:].astype(F32)
            value, slope = gelu_parts(gate)
            out_ref[pair, :, :TILE] = (grad * upper * slope).astype(LOW)
            out_ref[pair, :, TILE:] = (grad * value).astype(LOW)

    both = both_spec(rows, 2 * TILE)
    return pl.pallas_call(
        kernel,
        grid=(columns // TILE,),
        in_specs=[whole(x.shape), both, both_spec(D, TILE, at)],
        out_specs=both,
        out_shape=jax.ShapeDtypeStruct(gated.shape, LOW),
        compiler_params=params(),
        cost_estimate=cost(),
    )(x, gated, matrix)


def cols_sum(value_ref, matrix_ref):
    return dot_nt(value_ref[0], matrix_ref[0]) + dot_nt(value_ref[1], matrix_ref[1])


def norm_out(value, scale_ref, resid_ref, rows_ref):
    images = scale_ref.shape[0]
    resid_ref[...] = value
    for i in range(images):
        span = slice(i * SEQ, (i + 1) * SEQ)
        part = resid_ref[span, :]
        rows_ref[span, :] = (rms_norm(part) * scale_ref[i : i + 1, :]).astype(LOW)


def norm_grad(resid, scale, grad):
    root = lax.rsqrt(jnp.mean(resid * resid, axis=-1, keepdims=True) + NORM_EPS)
    normed = resid * root
    inner = grad * scale
    back = root * (inner - normed * jnp.mean(inner * normed, axis=-1, keepdims=True))
    return back, jnp.sum(grad * normed, axis=0, keepdims=True)


def cols_forward(value, matrix, width, at, resid, scale):
    _, rows, columns = value.shape
    steps = columns // width

    def kernel(value_ref, resid_ref, scale_ref, matrix_ref, out_ref, rows_ref, acc_ref):
        @pl.when(pl.program_id(0) == 0)
        def _():
            acc_ref[...] = resid_ref[...]

        acc_ref[...] += cols_sum(value_ref, matrix_ref)

        @pl.when(pl.program_id(0) == steps - 1)
        def _():
            norm_out(acc_ref[...], scale_ref, out_ref, rows_ref)

    return pl.pallas_call(
        kernel,
        grid=(steps,),
        in_specs=[
            both_spec(rows, width),
            whole(resid.shape),
            whole(scale.shape),
            both_spec(D, width, at),
        ],
        out_specs=[whole(resid.shape), whole(resid.shape)],
        out_shape=[
            jax.ShapeDtypeStruct(resid.shape, F32),
            jax.ShapeDtypeStruct(resid.shape, LOW),
        ],
        scratch_shapes=[pltpu.VMEM(resid.shape, F32)],
        compiler_params=params(),
        cost_estimate=cost(),
    )(value, resid, scale, matrix)


def cols_backward(value, matrix, width, at, resid, scale, grad, types):
    _, rows, columns = value.shape
    steps = columns // width

    def kernel(value_ref, resid_ref, scale_ref, grad_ref, matrix_ref, scale_out, *outs):
        *outs, acc_ref = outs

        @pl.when(pl.program_id(0) == 0)
        def _():
            acc_ref[...] = cols_sum(value_ref, matrix_ref)

        @pl.when(pl.program_id(0) > 0)
        def _():
            acc_ref[...] += cols_sum(value_ref, matrix_ref)

        @pl.when(pl.program_id(0) == steps - 1)
        def _():
            for i in range(scale_ref.shape[0]):
                span = slice(i * SEQ, (i + 1) * SEQ)
                back, scale_out[i : i + 1, :] = norm_grad(
                    resid_ref[span, :], scale_ref[i : i + 1, :], acc_ref[span, :]
                )
                back = back + grad_ref[span, :]
                for out in outs:
                    out[span, :] = back.astype(out.dtype)

    return pl.pallas_call(
        kernel,
        grid=(steps,),
        in_specs=[
            both_spec(rows, width),
            whole(resid.shape),
            whole(scale.shape),
            whole(resid.shape),
            both_spec(D, width, at),
        ],
        out_specs=[whole(scale.shape)] + [whole(resid.shape)] * len(types),
        out_shape=[jax.ShapeDtypeStruct(scale.shape, F32)]
        + [jax.ShapeDtypeStruct(resid.shape, kind) for kind in types],
        scratch_shapes=[pltpu.VMEM(resid.shape, F32)],
        compiler_params=params(),
        cost_estimate=cost(),
    )(value, resid, scale, grad, matrix)


def weight_grads(from_own, first, *pairs):
    rows, depth = pairs[0][0].shape
    half = depth // 2
    quarter = half // 2
    tiles = [value.shape[2] // TILE for _, value in pairs]
    starts = [sum(tiles[:i]) for i in range(len(tiles))]
    columns = sum(tiles) * TILE

    def kernel(*refs):
        count = len(pairs)
        order_ref, first_ref, *refs = refs
        x_refs, value_refs = refs[:count], refs[count : 2 * count]
        own_ref, *parts = refs[2 * count : 2 * count + 5]
        turned = refs[2 * count + 5 :]
        step = pl.program_id(0)
        for i in range(count):

            @pl.when(step == starts[i])
            def _():
                turned[i][...] = dot_nt(order_ref[...], x_refs[i][...]).astype(LOW)

            @pl.when((step >= starts[i]) & (step < starts[i] + tiles[i]))
            def _():
                for pair in range(2):
                    value = value_refs[i][first_ref[0] ^ pair]
                    own_ref[pair] = dot_f32(turned[i][:half, :], value).astype(LOW)
                    other = dot_f32(turned[i][half:, :], value).astype(LOW)
                    parts[2 * pair][...] = other[:quarter]
                    parts[2 * pair + 1][...] = other[quarter:]

    def value_spec(i):
        return pl.BlockSpec(
            (2, rows, TILE), lambda j: (0, 0, jnp.clip(j - starts[i], 0, tiles[i] - 1))
        )

    return pl.pallas_call(
        kernel,
        grid=(columns // TILE,),
        in_specs=[whole(from_own.shape), pl.BlockSpec(memory_space=pltpu.SMEM)]
        + [whole(x.shape) for x, _ in pairs]
        + [value_spec(i) for i in range(len(pairs))],
        out_specs=[pl.BlockSpec((2, half, TILE), lambda j: (0, 0, j))]
        + [pl.BlockSpec((quarter, TILE), lambda j: (0, j))] * 4,
        out_shape=[jax.ShapeDtypeStruct((2, half, columns), LOW)]
        + [jax.ShapeDtypeStruct((quarter, columns), LOW)] * 4,
        scratch_shapes=[pltpu.VMEM((depth, rows), LOW) for _ in pairs],
        compiler_params=params(),
        cost_estimate=cost(),
    )(from_own, first, *(x for x, _ in pairs), *(value for _, value in pairs))


def patch_weight_grads(*pairs):
    depth, columns = pairs[0][0].shape[1], pairs[0][1].shape[1]
    size = depth // 8

    def kernel(*refs):
        lefts, rights = refs[: len(pairs)], refs[len(pairs) : 2 * len(pairs)]
        own_ref, *parts = refs[2 * len(pairs) :]
        for i in range(len(pairs)):
            grad = dot_tn(lefts[i][...], rights[i][...]).astype(LOW)
            span = slice(i * columns, (i + 1) * columns)
            own_ref[0, :, span] = grad[: 2 * size]
            own_ref[1, :, span] = grad[2 * size : 4 * size]
            for j, part in enumerate(parts):
                part[:, span] = grad[(4 + j) * size : (5 + j) * size]

    width = len(pairs) * columns
    return pl.pallas_call(
        kernel,
        out_shape=[jax.ShapeDtypeStruct((2, 2 * size, width), LOW)]
        + [jax.ShapeDtypeStruct((size, width), LOW)] * 4,
        compiler_params=params(),
        cost_estimate=cost(),
    )(*(left for left, _ in pairs), *(right for _, right in pairs))


def head_part(ref, part):
    return ref[0, :, part * HEAD_DIM : (part + 1) * HEAD_DIM]


def softmax_turned(queries, keys):
    scores = dot_nt(keys, queries) * (1.0 / math.sqrt(HEAD_DIM))
    scores = jnp.exp(scores - jnp.max(scores, axis=0, keepdims=True))
    return scores * (1.0 / jnp.sum(scores, axis=0, keepdims=True))


def attention_specs(width):
    return [
        pl.BlockSpec((1, SEQ, width), lambda i, j, part=part: (i, j, part)) for part in range(3)
    ]


def attention_forward(project, width):
    rows = project.shape[1]

    def kernel(q_ref, k_ref, v_ref, out_ref):
        for part in range(width // HEAD_DIM):
            scores = dot_nt(head_part(q_ref, part), head_part(k_ref, part))
            scores = scores * (1.0 / math.sqrt(HEAD_DIM))
            scores = jnp.exp(scores - jnp.max(scores, axis=-1, keepdims=True))
            probs = scores * (1.0 / jnp.sum(scores, axis=-1, keepdims=True))
            mixed = dot_f32(probs.astype(LOW), head_part(v_ref, part))
            out_ref[0, :, part * HEAD_DIM : (part + 1) * HEAD_DIM] = mixed.astype(LOW)

    return pl.pallas_call(
        kernel,
        grid=(2, rows // SEQ),
        in_specs=attention_specs(width),
        out_specs=pl.BlockSpec((1, SEQ, width), lambda i, j: (i, j, 0)),
        out_shape=jax.ShapeDtypeStruct((2, rows, width), LOW),
        compiler_params=params(),
        cost_estimate=cost(8 * rows * SEQ * width, 16 * rows * width),
    )(project, project, project)


def attention_backward(project, grad, width):
    rows = project.shape[1]
    inverse_root = 1.0 / math.sqrt(HEAD_DIM)

    def kernel(q_ref, k_ref, v_ref, grad_ref, out_ref):
        for part in range(width // HEAD_DIM):
            queries, keys = head_part(q_ref, part), head_part(k_ref, part)
            values, grad = head_part(v_ref, part), head_part(grad_ref, part)
            probs = softmax_turned(queries, keys)
            grad_values = dot_f32(probs.astype(LOW), grad)
            grad_probs = dot_nt(values, grad)
            inner = jnp.sum(grad_probs * probs, axis=0, keepdims=True)
            grad_scores = (probs * (grad_probs - inner)).astype(LOW)
            grad_queries = dot_tn(keys, grad_scores).T * inverse_root
            grad_keys = dot_f32(grad_scores, queries) * inverse_root
            for place, value in enumerate((grad_queries, grad_keys, grad_values)):
                start = place * width + part * HEAD_DIM
                out_ref[0, :, start : start + HEAD_DIM] = value.astype(LOW)

    return pl.pallas_call(
        kernel,
        grid=(2, rows // SEQ),
        in_specs=attention_specs(width) + [pl.BlockSpec((1, SEQ, width), lambda i, j: (i, j, 0))],
        out_specs=pl.BlockSpec((1, SEQ, 3 * width), lambda i, j: (i, j, 0)),
        out_shape=jax.ShapeDtypeStruct((2, rows, 3 * width), LOW),
        compiler_params=params(),
        cost_estimate=cost(20 * rows * SEQ * width, 28 * rows * width),
    )(project, project, project, grad)


def loss_kernel(last, patch_out, target, coef, resid, scale):
    rows = last.shape[0]
    images = scale.shape[0]

    def kernel(
        last_ref, out_ref, target_ref, coef_ref, resid_ref, scale_ref,
        loss_ref, low_ref, grad_ref, rows_ref, scale_out,
    ):
        for i in range(images):
            span = slice(i * SEQ, (i + 1) * SEQ)
            diff = dot_nt(last_ref[span, :], out_ref[...]) - target_ref[span, :]
            total = jnp.sum(jnp.sum(diff * diff, axis=1, keepdims=True), axis=0, keepdims=True)
            loss_ref[i : i + 1, :] = jnp.broadcast_to(total, (1, 128))
            low = (diff * coef_ref[i : i + 1, :1]).astype(LOW)
            low_ref[span, :] = low
            back, scale_out[i : i + 1, :] = norm_grad(
                resid_ref[span, :], scale_ref[i : i + 1, :], dot_f32(low, out_ref[...])
            )
            grad_ref[span, :] = back
            rows_ref[span, :] = back.astype(LOW)

    return pl.pallas_call(
        kernel,
        out_shape=[
            jax.ShapeDtypeStruct((images, 128), F32),
            jax.ShapeDtypeStruct((rows, PD), LOW),
            jax.ShapeDtypeStruct((rows, D), F32),
            jax.ShapeDtypeStruct((rows, D), LOW),
            jax.ShapeDtypeStruct((images, D), F32),
        ],
        compiler_params=params(),
        cost_estimate=cost(4 * rows * D * PD, 16 * rows * D),
    )(last, patch_out, target, coef, resid, scale)


def body(
    clean_images,
    noise_draw,
    levels,
    labels,
    dropped,
    groups,
    step_count,
    inward,
    first_inward,
    second_inward,
    outward,
    first_outward,
    second_outward,
    expand,
    first_expand,
    second_expand,
    shrink,
    first_shrink,
    second_shrink,
    patches,
    first_patches,
    second_patches,
    classes,
    first_classes,
    second_classes,
    mapping,
    first_mapping,
    second_mapping,
):
    masters = (inward, outward, expand, shrink, patches, classes, mapping)
    firsts = (
        first_inward,
        first_outward,
        first_expand,
        first_shrink,
        first_patches,
        first_classes,
        first_mapping,
    )
    seconds = (
        second_inward,
        second_outward,
        second_expand,
        second_shrink,
        second_patches,
        second_classes,
        second_mapping,
    )
    links = Links(lax.axis_size("dp"))
    me, pair = lax.axis_index("dp"), lax.axis_index("tensor")
    own_place = me * 2 + pair
    images = clean_images.shape[0]
    rows = images * SEQ
    width = inward.shape[2]
    ff_width = expand.shape[2]
    ff_tiles = ff_width // TILE
    map_rows = mapping.shape[0]

    have = types.SimpleNamespace()
    rounds = Rounds(have)

    def turn(*values):
        return values[0] if len(values) == 1 else values

    flat_patch = jnp.concatenate([patches[0], patches[1]], axis=1).astype(LOW)
    table = jnp.pad(classes.T, ((0, 0), (0, TABLE - CLASSES)))
    flat_map = jnp.concatenate([table, mapping], axis=1).astype(LOW)
    flat_up = expand.reshape(-1, 2, ff_tiles, TILE).transpose(0, 2, 1, 3)
    flat = jnp.concatenate(
        [
            flat_up.reshape(expand.shape[0], -1),
            shrink.T,
            inward.reshape(inward.shape[0], -1),
            outward.T,
        ],
        axis=1,
    ).astype(LOW)
    block = lax.all_gather(flat, ("tensor", "dp"), axis=0, tiled=True)
    block = block.reshape(2, D, flat.shape[1])
    at_down = 2 * ff_tiles
    at_in = 3 * ff_tiles
    at_out = at_in + 3 * width // TILE
    g_p = Run(links.gather(flat_patch))
    g_m = Run(links.gather_rows(flat_map, (1,), (None,), (0,)))
    s_p, s_a, s_e, s_s, rows_run = (Run() for _ in range(5))
    line = links.size // 4
    part = 8 * map_rows

    n_up = len(links.upper)

    order_d = spread([reverse_bits(i, links.bits) for i in range(links.size)], me, D // links.size)
    to_own = order_matrix(D, order_d)
    from_own = to_own.T
    this_pair = pair.reshape(1)
    places = []
    for i in range(2 * links.size):
        place = 0
        for bit, step in enumerate(links.upper):
            place |= ((i >> bit) & 1) << (step + 1)
        place |= ((i >> n_up) & 1) << 2
        place |= (i >> (n_up + 1)) & 1
        place |= ((i >> (n_up + 2)) & 1) << 1
        places.append(place)
    order_p = spread(places, own_place, map_rows)
    to_own_p = order_matrix(PD, order_p)

    sigma, radius, _ = noise_terms(levels)
    chosen = jnp.where(dropped == 1, CLASSES - 1, labels)
    sig = jnp.repeat(sigma, SEQ)[:, None]
    rad = jnp.repeat(radius, SEQ)[:, None]
    clean_float = dot_f32(clean_images.reshape(rows, PD), to_own_p)
    noise_float = dot_f32(noise_draw.reshape(rows, PD), to_own_p)
    inputs = ((clean_float + sig * noise_float) / rad).astype(LOW)
    target = (sig * clean_float - SIGMA_DATA * SIGMA_DATA * noise_float) / (SIGMA_DATA * rad)
    counts = jnp.sum((groups[:, None] == groups[None, :]).astype(F32), axis=1)
    weight = 1.0 / (GROUPS * counts)

    coef = jnp.broadcast_to((2.0 * weight / (SEQ * PD))[:, None], (images, 128))


    def in_order(values, axis):
        found = []
        for i in range(line):
            index = links.index(i ^ (me // 4))
            found.append(sum(jnp.where(index == j, v, 0) for j, v in enumerate(values)))
        return jnp.concatenate(found, axis=axis)

    def cut_for_line(value):
        return [
            lax.dynamic_slice_in_dim(value, ((me // 4) ^ links.place(i)) * part, part, axis=1)
            for i in range(line)
        ]

    def seen(values):
        shape = (line, images, -1)
        return sum(
            links.seen_from_here(value.reshape(shape), i) for i, value in enumerate(values)
        ).reshape(line * images, -1)

    def run_names():
        names = jnp.stack([chosen, levels], axis=1)
        have.names = links.along([turn(names)] * line)

    def run_cond():
        names = jnp.concatenate(have.names, axis=0)
        have.chosen, have.levels = names[:, 0], names[:, 1]
        have.feats_low = noise_terms(have.levels)[2].astype(LOW)
        onehot = (have.chosen[:, None] == jnp.arange(TABLE)[None, :]).astype(LOW)
        known = jnp.concatenate([onehot, have.feats_low], axis=1)
        places = [((i & 1) << 2) | ((i >> 1) & 1) | ((i >> 2) << 1) for i in range(8)]
        order_m = order_matrix(part, spread(places, own_place % 8, map_rows))
        map_part = dot_f32(order_m, g_m.finish()).astype(LOW)
        have.map_in = map_part[:, TABLE + FOUR : TABLE + FOUR + CD]
        have.map_out = map_part[:, TABLE + FOUR + CD :]
        have.cond_zero = dot_nt(known, map_part[:, : TABLE + FOUR])
        squares = jnp.sum(have.cond_zero * have.cond_zero, axis=1, keepdims=True)
        squares = turn(jnp.broadcast_to(squares, (line * images, 128)))
        have.squares = links.along([squares] * line)

    def run_inner():
        squares = seen(turn(*have.squares))[:, :1]
        have.root = lax.rsqrt(squares * (1.0 / CD) + NORM_EPS)
        have.normed = (have.cond_zero * have.root).astype(LOW)
        have.inners = links.along(turn(*cut_for_line(dot_f32(have.normed, have.map_in))))

    def run_scales():
        have.inner = seen(turn(*have.inners))
        have.cond_low = (have.cond_zero + jax.nn.gelu(have.inner)).astype(LOW)
        scales = dot_f32(have.cond_low, have.map_out)
        scales = turn(*(scales[i * images : (i + 1) * images] for i in range(line)))
        have.scale_parts = links.along(scales)

    def run_map():
        scales = 1.0 + sum(turn(*have.scale_parts))
        have.scales = scales.reshape(images, 3, D)

    def run_patch():
        have.patch_all = assemble(g_p.finish())
        have.resid_zero = dot_f32(inputs, have.patch_all[:, :D])

    def run_in():
        rows_zero = rms_norm(have.resid_zero) * jnp.repeat(have.scales[:, 0], SEQ, axis=0)
        have.rows_zero = rows_zero.astype(LOW)
        have.project = rows_matmul(have.rows_zero, block, 3 * width, at_in)

    def run_mix():
        have.mixed = turn(attention_forward(have.project, width))

    def run_out():
        have.resid_one, have.rows_one = cols_forward(
            have.mixed, block, TILE, at_out, have.resid_zero, have.scales[:, 1]
        )

    def run_up():
        have.gated, have.hidden = expand_forward(have.rows_one, block, 2 * ff_width)

    def run_down():
        have.resid_two, have.last = cols_forward(
            have.hidden, block, TILE, at_down, have.resid_one, have.scales[:, 2]
        )

    def run_loss():
        have.squared, have.grad_low, have.grad_two, have.rows_two, have.scale_two = loss_kernel(
            have.last, have.patch_all[:, D:], target, coef, have.resid_two, have.scales[:, 2]
        )

    def start(run, parts, groups=((0, 1, 2),)):
        run.begin(links.reduce(groups, *parts))

    def grad_down():
        start(s_s, weight_grads(from_own, this_pair, (have.rows_two, have.hidden)))

    def back_down():
        have.gated_grad = shrink_backward(have.rows_two, block, at_down, have.gated)

    def grad_up():
        parts = weight_grads(from_own, this_pair, (have.rows_one, have.gated_grad))
        start(s_e, parts, ((0,), (1, 2)))

    def back_up():
        have.scale_one, have.grad_one, have.rows_grad = cols_backward(
            have.gated_grad, block, 2 * TILE, 0, have.resid_one, have.scales[:, 1],
            have.grad_two, (F32, LOW),
        )

    def back_out():
        have.grad_mixed = rows_matmul(have.rows_grad, block, width, at_out)

    def back_mix():
        have.grad_project = attention_backward(have.project, have.grad_mixed, width)

    def grad_in():
        start(
            s_a,
            weight_grads(
                from_own, this_pair,
                (have.rows_zero, have.grad_project), (have.rows_grad, have.mixed),
            ),
        )

    def back_in():
        have.scale_zero, have.grad_zero = cols_backward(
            have.grad_project, block, TILE, at_in, have.resid_zero, have.scales[:, 0],
            have.grad_one, (LOW,),
        )

    def grad_patch():
        pairs = ((inputs, have.grad_zero), (have.grad_low, have.last))
        start(s_p, patch_weight_grads(*pairs))

    def back_map():
        grad_scales = jnp.stack([have.scale_zero, have.scale_one, have.scale_two], axis=1)
        scales_low = grad_scales.reshape(images, 3 * D).astype(LOW)
        have.scale_grads = links.along([turn(scales_low)] * line)

    def back_scales():
        have.scales_low = jnp.concatenate(turn(*have.scale_grads), axis=0)
        have.grad_cond = dot_nt(have.scales_low, have.map_out)
        _, pull_gelu = jax.vjp(jax.nn.gelu, have.inner)
        (grad_inner,) = pull_gelu(have.grad_cond)
        low = grad_inner.astype(LOW)
        inner = jnp.sum(low.astype(F32) * have.inner, axis=1, keepdims=True)
        have.inner_grads = links.along([low] * line)
        have.sums = links.along([jnp.broadcast_to(inner, (line * images, 128))] * line)

    def back_cond():
        grads = [
            links.seen_from_here(grad.reshape(line, images, part), i)
            for i, grad in enumerate(have.inner_grads)
        ]
        have.inner_low = in_order(grads, 2).reshape(line * images, CD)
        grad_normed = dot_nt(have.inner_low, have.map_in)
        mean = seen(have.sums)[:, :1] * (1.0 / CD)
        zero = have.root * (grad_normed - have.cond_zero * have.root * mean) + have.grad_cond
        code = jnp.stack([have.chosen // 32, have.chosen % 32], axis=1).astype(LOW)
        code = jnp.pad(code, ((0, 0), (0, 126)))
        sent = (
            have.scales_low, have.inner_low, have.feats_low, code,
            zero.astype(LOW), have.normed, have.cond_low,
        )
        rows_run.begin(links.gather_rows(jnp.concatenate(sent, axis=1)[None], (0, 1), (None,)))

    def grad_map():
        all_rows = rows_run.finish()
        all_rows = all_rows.reshape(-1, all_rows.shape[2])
        starts = [0]
        for size in (3 * D, CD, FOUR, 128, part, part, part):
            starts.append(starts[-1] + size)
        scales_all, inner_all, feats_all, code_all, zero_all, normed_all, cond_all = (
            all_rows[:, a:b] for a, b in zip(starts[:-1], starts[1:])
        )
        first = (own_place % 8) * map_rows
        pick = jnp.arange(part)[:, None] == first + jnp.arange(map_rows)[None, :]
        pick = pick.astype(LOW)
        zero_own = dot_f32(zero_all, pick).astype(LOW)
        normed_own = dot_f32(normed_all, pick).astype(LOW)
        cond_own = dot_f32(cond_all, pick).astype(LOW)
        code_all = code_all.astype(jnp.int32)
        chosen_all = code_all[:, 0] * 32 + code_all[:, 1]
        onehot_all = (chosen_all[:, None] == jnp.arange(CLASSES)[None, :]).astype(LOW)
        have.table_grad = dot_tn(onehot_all, zero_own)
        have.mapping_grad = jnp.concatenate(
            [
                dot_tn(zero_own, feats_all),
                dot_tn(normed_own, inner_all),
                dot_tn(cond_own, scales_all),
            ],
            axis=1,
        )

    def more_p():
        s_p.go_on()

    def more_r():
        rows_run.go_on()

    for runs, works, held in (
        ((g_p, g_m), (run_names,), ()),
        ((g_p, g_m), (), ()),
        ((g_p, g_m), (), ()),
        ((g_p,), (run_cond,), ()),
        ((), (run_inner, run_patch), ()),
        ((), (run_scales,), ()),
        ((), (run_map,), ()),
        ((), (run_in,), ()),
        ((), (run_mix,), ()),
        ((), (run_out,), ()),
        ((), (run_up,), ()),
        ((), (run_down,), ()),
        ((), (run_loss,), ()),
        ((), (grad_down,), ()),
        ((s_s,), (back_down,), ()),
        ((s_s,), (grad_up,), ()),
        ((s_s, s_e), (back_up, back_out), ()),
        ((s_e,), (back_mix, grad_in), ()),
        ((s_e, s_a, s_s), (back_in, back_map, grad_patch), ()),
        ((s_a, s_p, s_e), (back_scales, more_p), (s_s,)),
        ((s_a, s_e, s_p), (), ()),
        ((s_a, s_p), (back_cond, more_r), (s_e,)),
        ((rows_run,), (), ()),
        ((s_a, s_p, s_e, s_s), (grad_map,), ()),
    ):
        rounds(runs, works, held)
    patch_grads = s_p.finish()
    attn_grads = s_a.finish()
    up_grad = s_e.finish().reshape(-1, ff_tiles, 2, TILE).transpose(0, 2, 1, 3)
    grads = (
        attn_grads[:, : 3 * width].reshape(inward.shape),
        attn_grads[:, 3 * width :].T,
        up_grad.reshape(expand.shape),
        s_s.finish().T,
        jnp.stack([patch_grads[:, :D], patch_grads[:, D:]]),
        have.table_grad,
        have.mapping_grad,
    )
    squares = sum((jnp.sum(grad * grad) for grad in grads))
    local_loss = jnp.sum(weight * have.squared[:, 0]) / (SEQ * PD)
    sums = links.total(jnp.stack([local_loss, squares]))
    sums = sums + rounds.token[0, :2]
    total_loss = sums[0]
    grad_norm = jnp.sqrt(sums[1])
    factor = CLIP / (grad_norm + NORM_EPS)
    count = step_count[0].astype(F32)
    fix_one = 1.0 - jnp.power(BETA_ONE, count)
    fix_two = 1.0 - jnp.power(BETA_TWO, count)
    results = [total_loss, grad_norm]
    for master, first, second, grad in zip(masters, firsts, seconds, grads):
        clipped = grad * factor
        moment = BETA_ONE * first + (1.0 - BETA_ONE) * clipped
        square = BETA_TWO * second + (1.0 - BETA_TWO) * clipped * clipped
        step_size = moment / fix_one / (jnp.sqrt(square / fix_two) + ADAM_EPS)
        results.extend([master - LEARN_RATE * (step_size + DECAY * master), moment, square])
    return tuple(results)


def solution(mesh):
    in_specs = (
        P(("dp", "tensor"), None, None),
        P(("dp", "tensor"), None, None),
        P(("dp", "tensor")),
        P(("dp", "tensor")),
        P(("dp", "tensor")),
        P(("dp", "tensor")),
        P(),
        P("dp", None, "tensor"),
        P("dp", None, "tensor"),
        P("dp", None, "tensor"),
        P("tensor", "dp"),
        P("tensor", "dp"),
        P("tensor", "dp"),
        P("dp", None, "tensor"),
        P("dp", None, "tensor"),
        P("dp", None, "tensor"),
        P("tensor", "dp"),
        P("tensor", "dp"),
        P("tensor", "dp"),
        P(None, ("dp", "tensor"), None),
        P(None, ("dp", "tensor"), None),
        P(None, ("dp", "tensor"), None),
        P(None, ("dp", "tensor")),
        P(None, ("dp", "tensor")),
        P(None, ("dp", "tensor")),
        P(("dp", "tensor"), None),
        P(("dp", "tensor"), None),
        P(("dp", "tensor"), None),
    )
    out_specs = (
        P(),
        P(),
        P("dp", None, "tensor"),
        P("dp", None, "tensor"),
        P("dp", None, "tensor"),
        P("tensor", "dp"),
        P("tensor", "dp"),
        P("tensor", "dp"),
        P("dp", None, "tensor"),
        P("dp", None, "tensor"),
        P("dp", None, "tensor"),
        P("tensor", "dp"),
        P("tensor", "dp"),
        P("tensor", "dp"),
        P(None, ("dp", "tensor"), None),
        P(None, ("dp", "tensor"), None),
        P(None, ("dp", "tensor"), None),
        P(None, ("dp", "tensor")),
        P(None, ("dp", "tensor")),
        P(None, ("dp", "tensor")),
        P(("dp", "tensor"), None),
        P(("dp", "tensor"), None),
        P(("dp", "tensor"), None),
    )
    return jax.shard_map(body, mesh=mesh, in_specs=in_specs, out_specs=out_specs, check_vma=False)
```
